128 devices in a mesh: dp: 8 (over x, core), fsdp: 16 (over y, z).
Axes of the slice: x: 4, y: 4, z: 4, core: 2. Of those that a mesh axis runs over, the one named last changes fastest.
Arguments:
- rollout_hidden: bfloat16 [65536, 5120], P(('dp', 'fsdp')), may hold values from -64 to 64
- key_weight: bfloat16 [5120, 512], P('fsdp'), may hold values from -0.078125 to 0.078125
- value_weight: bfloat16 [5120, 512], P('fsdp'), may hold values from -0.078125 to 0.078125
- key_gain: float32 [128], replicated, may hold values from 0.1 to 1.9
- query_gain: float32 [128], replicated, may hold values from 0.1 to 1.9
- queries: bfloat16 [65536, 4096], P(('dp', 'fsdp')), may hold values from -64 to 64
- out_grad: bfloat16 [65536, 4096], P(('dp', 'fsdp')), may hold values from -6 to 6
- rewards: float32 [16, 8], P('fsdp'), may hold values from -4 to 4
- response_lengths: int32 [16, 8], P('fsdp'), may hold values from 256 to 512, as said below
- rollout_owner: int32 [16, 8], P('fsdp'), may hold values from 0 to 7, as said below
- train_shard: int32 [16, 8], P('fsdp'), may hold values from 0 to 7, as said below
- pack_offsets: int32 [16, 8], P('fsdp'), may hold values from 0 to 0, as said below
Outputs:
- d_hidden: bfloat16 [65536, 5120], P(('dp', 'fsdp'))
- d_queries: bfloat16 [65536, 4096], P(('dp', 'fsdp'))
- grad_key_weight: float32 [5120, 512], P('fsdp')
- grad_value_weight: float32 [5120, 512], P('fsdp')
- grad_query_gain: float32 [128], replicated
- grad_key_gain: float32 [128], replicated
The draws below stay inside these ranges and needn't reach their ends.
Inputs may be any that keep to these rules, and one draw needn't show every extreme that they name: `response_lengths`: in every column at least one response is 512 long. `rollout_owner`: in every column each dp index generated exactly one response, and no two responses of a column generated by different dp indices go to the same training shard. `train_shard`: in every column each dp index trains exactly 1 responses. `pack_offsets`: multiples of 512; the responses that one dp index trains in one column have distinct offsets.
All inputs are finite; a program needn't handle non-finite values.
Results may differ from the reference program's by a relative error of at most 0.03.
Values may be sent and summed in bfloat16 or wider, within the bound.
A program may use at most 256 MiB of HBM per device.

```python
import math
import jax
import jax.numpy as jnp
from jax import lax

D = 5120
QH = 32
KVH = 4
HD = 128
GSIZE = 4
TILE = 512
SLOTS = 1
TOK_DEV = 512
RESP_COL = 8
N_DP = 8
N_FSDP = 16


def column_layout(key):
    key_resp, key_cycle, key_slot, key_len, key_long = jax.random.split(key, 5)
    resp_count = SLOTS * N_DP
    response = jax.random.permutation(key_resp, resp_count).astype(jnp.int32)
    cycle_order = jax.random.permutation(key_cycle, N_DP).astype(jnp.int32)
    cell_index = jnp.arange(resp_count, dtype=jnp.int32)
    owner_cell = cell_index // SLOTS
    slot_cell = cell_index % SLOTS
    trainer_cell = (owner_cell + cycle_order[slot_cell % N_DP]) % N_DP
    slot_keys = jax.random.split(key_slot, N_DP)
    slot_order = jax.vmap(lambda slot_key: jax.random.permutation(slot_key, SLOTS))(slot_keys).astype(jnp.int32)
    pack_cell = slot_order[trainer_cell, slot_cell]
    lengths = jax.random.randint(key_len, (resp_count,), TILE // 2, TILE + 1, dtype=jnp.int32)
    longest = jax.random.randint(key_long, (), 0, resp_count, dtype=jnp.int32)
    lengths = lengths.at[longest].set(TILE)
    owner_of = jnp.zeros((resp_count,), jnp.int32).at[response].set(owner_cell)
    trainer = jnp.zeros((resp_count,), jnp.int32).at[response].set(trainer_cell)
    offset = jnp.zeros((resp_count,), jnp.int32).at[response].set(pack_cell * TILE)
    return (lengths, owner_of, trainer, offset)


def all_layouts(key):
    return jax.vmap(column_layout)(jax.random.split(key, N_FSDP))


def draw_response_lengths(key, part):
    return all_layouts(key)[0]


def draw_rollout_owner(key, part):
    return all_layouts(key)[1]


def draw_train_shard(key, part):
    return all_layouts(key)[2]


def draw_pack_offsets(key, part):
    return all_layouts(key)[3]


def draw_rollout_hidden(key, part):
    key = jax.random.fold_in(key, 11)
    key_entry, key_row, key_col = jax.random.split(key, 3)
    row_count = N_DP * N_FSDP * SLOTS * TILE
    col_scale = jnp.exp(jax.random.uniform(key_col, (1, D), jnp.float32, -0.7, 0.7))
    entry = jax.random.normal(key_entry, (row_count, D), jnp.float32)
    row_scale = jnp.exp(jax.random.uniform(key_row, (row_count, 1), jnp.float32, -1.15, 1.15))
    return (entry * row_scale * col_scale).astype(jnp.bfloat16)


def draw_queries(key, part):
    key = jax.random.fold_in(key, 12)
    key_entry, key_row, key_col = jax.random.split(key, 3)
    row_count = N_DP * N_FSDP * SLOTS * TILE
    col_scale = jnp.exp(jax.random.uniform(key_col, (1, QH * HD), jnp.float32, -0.7, 0.7))
    entry = jax.random.normal(key_entry, (row_count, QH * HD), jnp.float32)
    row_scale = jnp.exp(jax.random.uniform(key_row, (row_count, 1), jnp.float32, -1.15, 1.15))
    return (entry * row_scale * col_scale).astype(jnp.bfloat16)


def block_scale(stream_key, dims, cuts, smallest, largest):
    loudness, own = 1.0, jax.random.fold_in(stream_key, 6)
    for dim, blocks in cuts:
        steps = jnp.exp(jax.random.uniform(jax.random.fold_in(own, dim), (blocks,), jnp.float32, smallest / len(cuts), largest / len(cuts)))
        loudness = loudness * jnp.repeat(steps, dims[dim] // blocks).reshape([-1 if axis == dim else 1 for axis in range(len(dims))])
    return loudness


def normal_values(own_key, shape, spread, reach, cuts=(), kind=jnp.bfloat16):
    entries = spread * jax.random.normal(own_key, shape, jnp.float32)
    if cuts:
        entries = entries * block_scale(own_key, shape, cuts, -0.22, 0.18)
    return jnp.clip(entries, -reach, reach).astype(kind)


def setup_inputs(seed: int = 0) -> dict:
    arg_keys = jax.random.split(jax.random.key(seed), 13)
    return {
        "rollout_hidden": draw_rollout_hidden(jax.random.fold_in(arg_keys[12], 71), 0),
        "key_weight": normal_values(arg_keys[1], (D, KVH * HD), D ** -0.5, 0.078125, ((0, 16),)),
        "value_weight": normal_values(arg_keys[2], (D, KVH * HD), D ** -0.5, 0.078125, ((0, 16),)),
        "key_gain": jnp.clip(1.0 + 0.18 * jax.random.normal(arg_keys[3], (HD,), jnp.float32), 0.1, 1.9),
        "query_gain": jnp.clip(1.0 + 0.18 * jax.random.normal(arg_keys[4], (HD,), jnp.float32), 0.1, 1.9),
        "queries": draw_queries(jax.random.fold_in(arg_keys[12], 71), 0),
        "out_grad": normal_values(arg_keys[6], (N_DP * N_FSDP * TOK_DEV, QH * HD), 1.0, 6.0, ((0, 128),)),
        "rewards": normal_values(arg_keys[7], (N_FSDP, RESP_COL), 1.0, 4.0, ((0, 16),), jnp.float32),
        "response_lengths": draw_response_lengths(jax.random.fold_in(arg_keys[12], 71), 0),
        "rollout_owner": draw_rollout_owner(jax.random.fold_in(arg_keys[12], 71), 0),
        "train_shard": draw_train_shard(jax.random.fold_in(arg_keys[12], 71), 0),
        "pack_offsets": draw_pack_offsets(jax.random.fold_in(arg_keys[12], 71), 0),
    }


eps_norm = 1e-06
rope_base = 1000000.0

def rope_tables(length, head_width):
    half_width = head_width // 2
    position = jnp.arange(length).astype(jnp.float32)
    frequency = rope_base ** (-jnp.arange(half_width).astype(jnp.float32) / half_width)
    angles = position[:, None] * frequency[None, :]
    return (jnp.cos(angles)[:, None, :], jnp.sin(angles)[:, None, :])

def rotate(vectors, cosine, sine_table):
    half_width = vectors.shape[-1] // 2
    first_half = vectors[..., :half_width]
    second_half = vectors[..., half_width:]
    return jnp.concatenate([first_half * cosine - second_half * sine_table, second_half * cosine + first_half * sine_table], axis=-1)

def unrotate(gradients, cosine, sine_table):
    half_width = gradients.shape[-1] // 2
    first_half = gradients[..., :half_width]
    second_half = gradients[..., half_width:]
    return jnp.concatenate([first_half * cosine + second_half * sine_table, second_half * cosine - first_half * sine_table], axis=-1)

def norm_forward(raw_values, gain_vector):
    inv_scale = lax.rsqrt(lax.optimization_barrier(jnp.mean(raw_values * raw_values, axis=-1, keepdims=True)) + eps_norm)
    unit_rows = raw_values * inv_scale
    return (unit_rows * gain_vector, unit_rows, inv_scale)

def norm_backward(grad_out, unit_rows, inv_scale, gain_vector):
    grad_unit = grad_out * gain_vector
    grad_in = inv_scale * (grad_unit - unit_rows * lax.optimization_barrier(jnp.mean(grad_unit * unit_rows, axis=-1, keepdims=True)))
    gain_part = lax.optimization_barrier(jnp.sum((grad_out * unit_rows).reshape(-1, unit_rows.shape[-1]), axis=0))
    return (grad_in, gain_part)

def earlier_equal(labels):
    order_index = jnp.arange(labels.shape[-1])
    earlier = order_index[None, :] < order_index[:, None]
    same_label = (labels[..., :, None] == labels[..., None, :]) & earlier
    return lax.optimization_barrier(jnp.sum(same_label.astype(jnp.int32), axis=-1)).astype(jnp.int32)

def to_low(values):
    return lax.optimization_barrier(values.astype(jnp.bfloat16)).astype(jnp.float32)

def tile_backward(query_tile, key_tile, value_tile, grad_tile, length, coefficient, query_gain, cosine, sine_table):
    tile_rows = key_tile.shape[0]
    group_size = QH // KVH
    inv_root = 1.0 / math.sqrt(HD)
    raw_query = query_tile.astype(jnp.float32).reshape(tile_rows, QH, HD)
    query_normed, query_unit, query_inv = norm_forward(raw_query, query_gain)
    query_rot = to_low(rotate(query_normed, cosine, sine_table)).reshape(tile_rows, KVH, group_size, HD)
    key_float = key_tile.astype(jnp.float32)
    value_float = value_tile.astype(jnp.float32)
    row_index = jnp.arange(tile_rows)
    allowed = (row_index[None, :] <= row_index[:, None]) & (row_index[None, :] < length)
    scores = jnp.einsum('ikgd,jkd->kgij', query_rot, key_float) * inv_root
    weight = jnp.where(allowed, jnp.exp(scores), 0.0)
    probability = weight / lax.optimization_barrier(jnp.sum(weight, axis=-1, keepdims=True))
    probs_low = to_low(probability)
    attended = to_low(jnp.einsum('kgij,jkd->ikgd', probs_low, value_float))
    live_rows = (row_index < length).astype(jnp.float32)
    scaled = to_low(coefficient * live_rows[:, None, None] * grad_tile.astype(jnp.float32).reshape(tile_rows, QH, HD))
    scaled = scaled.reshape(tile_rows, KVH, group_size, HD)
    grad_values = jnp.einsum('kgij,ikgd->jkd', probs_low, scaled).astype(jnp.bfloat16)
    grad_probs = jnp.einsum('ikgd,jkd->kgij', scaled, value_float)
    dotted = jnp.einsum('ikgd,ikgd->kgi', scaled, attended)
    grad_scores = to_low(probability * (grad_probs - dotted[..., None]))
    grad_query = jnp.einsum('kgij,jkd->ikgd', grad_scores, key_float) * inv_root
    grad_keys = (jnp.einsum('kgij,ikgd->jkd', grad_scores, query_rot) * inv_root).astype(jnp.bfloat16)
    grad_normed = unrotate(grad_query.reshape(tile_rows, QH, HD), cosine, sine_table)
    grad_raw, gain_part = norm_backward(grad_normed, query_unit, query_inv, query_gain)
    return (grad_raw.reshape(tile_rows, QH * HD).astype(jnp.bfloat16), gain_part, grad_keys, grad_values)

def reference(rollout_hidden, key_weight, value_weight, key_gain, query_gain, queries, out_grad, rewards, response_lengths, rollout_owner, train_shard, pack_offsets):
    column = jnp.arange(N_FSDP).astype(jnp.int32)[:, None]
    own_tile = ((rollout_owner * N_FSDP + column) * SLOTS + earlier_equal(rollout_owner)).reshape(-1).astype(jnp.int32)
    pack_tile = ((train_shard * N_FSDP + column) * SLOTS + pack_offsets // TILE).reshape(-1).astype(jnp.int32)
    grouped = rewards.reshape(N_FSDP, -1, GSIZE)
    advantage = (grouped - lax.optimization_barrier(jnp.mean(grouped, axis=-1, keepdims=True))).reshape(-1)
    lengths = response_lengths.reshape(-1)
    cosine, sine_table = rope_tables(TILE, HD)
    key_raw = jnp.dot(rollout_hidden, key_weight, preferred_element_type=jnp.float32)
    value_rows = jnp.dot(rollout_hidden, value_weight, preferred_element_type=jnp.float32).astype(jnp.bfloat16)
    tile_total = key_raw.shape[0] // TILE
    key_normed, key_unit, key_inv = norm_forward(key_raw.reshape(tile_total, TILE, KVH, HD), key_gain)
    key_rot = rotate(key_normed, cosine, sine_table).astype(jnp.bfloat16)
    value_tiles = value_rows.reshape(tile_total, TILE, KVH, HD)
    query_tiles = queries.reshape(tile_total, TILE, QH * HD)
    grad_tiles = out_grad.reshape(tile_total, TILE, QH * HD)

    def one_response(entry):
        source, target, length, coefficient = entry
        return tile_backward(query_tiles[target], key_rot[source], value_tiles[source], grad_tiles[target], length, coefficient, query_gain, cosine, sine_table)
    grad_query, query_parts, grad_keys, grad_values = lax.map(one_response, (own_tile, pack_tile, lengths, advantage))
    d_queries = jnp.zeros((tile_total, TILE, QH * HD), jnp.bfloat16).at[pack_tile].set(grad_query).reshape(-1, QH * HD)
    key_grad_tiles = jnp.zeros((tile_total, TILE, KVH, HD), jnp.bfloat16).at[own_tile].set(grad_keys)
    value_grad_rows = jnp.zeros((tile_total, TILE, KVH, HD), jnp.bfloat16).at[own_tile].set(grad_values).reshape(-1, KVH * HD)
    grad_key_normed = unrotate(key_grad_tiles.astype(jnp.float32), cosine, sine_table)
    grad_key_raw, grad_key_gain = norm_backward(grad_key_normed, key_unit, key_inv, key_gain)
    key_grad_rows = grad_key_raw.reshape(-1, KVH * HD).astype(jnp.bfloat16)
    d_hidden = (jnp.dot(key_grad_rows, key_weight.T, preferred_element_type=jnp.float32) + jnp.dot(value_grad_rows, value_weight.T, preferred_element_type=jnp.float32)).astype(jnp.bfloat16)
    grad_key_weight = jnp.dot(rollout_hidden.T, key_grad_rows, preferred_element_type=jnp.float32)
    grad_value_weight = jnp.dot(rollout_hidden.T, value_grad_rows, preferred_element_type=jnp.float32)
    grad_query_gain = lax.optimization_barrier(jnp.sum(query_parts, axis=0))
    return (d_hidden, d_queries, grad_key_weight, grad_value_weight, grad_query_gain, grad_key_gain)
```

```python
import functools
import math

import jax
import jax.numpy as jnp
import numpy as np
from jax import lax
from jax.experimental import pallas as pl
from jax.experimental.pallas import tpu as pltpu
from jax.sharding import PartitionSpec as P

MESH = pl.DeviceIdType.MESH
BF, F32 = jnp.bfloat16, jnp.float32
HD = 128
GSIZE = 4
TILE = 512
D = 5120
KVH = 4
QH = 32
GROUP = QH // KVH
NDP = 8
SHARD = 320
HALF = SHARD // 2
PIECE = TILE // NDP
EPS = 1e-06
VMEM_LIMIT = 60 * 1024 * 1024


def rope_arrays():
    half = HD // 2
    frequency = 1000000.0 ** (-np.arange(half, dtype=np.float64) / half)
    angles = np.arange(TILE, dtype=np.float64)[:, None] * frequency[None, :]
    cosine, sine = np.cos(angles), np.sin(angles)
    return (
        np.concatenate([cosine, cosine], axis=1).astype(np.float32),
        np.concatenate([-sine, sine], axis=1).astype(np.float32),
    )


def place():
    dp, fs = lax.axis_index("dp"), lax.axis_index("fsdp")
    return dp, fs, dp // 2, dp % 2, fs // 4, fs % 4


def remote(src, dst, send, recv, device):
    return pltpu.make_async_remote_copy(
        src_ref=src, dst_ref=dst, send_sem=send, recv_sem=recv, device_id=device, device_id_type=MESH
    )


def entry_barrier(peers):
    barrier = pltpu.get_barrier_semaphore()
    for peer in peers:
        pl.semaphore_signal(barrier, inc=1, device_id=peer, device_id_type=MESH)
    pl.semaphore_wait(barrier, len(peers))


def swap_lanes(values):
    return pltpu.roll(values, HD // 2, axis=1)


class Sends:
    def __init__(self):
        self.pending = []

    def start(self, *args):
        copy = remote(*args)
        copy.start()
        self.pending.append(copy)

    def drain(self):
        for copy in self.pending:
            copy.wait_send()
        self.pending = []


def skewed(stages, chunks, skew=1):
    for tick in range(len(stages) + skew * (chunks - 1)):
        for chunk in range(chunks):
            step = tick - skew * chunk
            if 0 <= step < len(stages):
                stages[step](chunk)


def gather_kernel(
    x_hbm, w_hbm, gain_ref, cos_ref, sin_ref, pick_ref,
    wfull_hbm, kv_hbm, raw_ref, xt_hbm,
    x_v, w_v, xt_v, tile_v, mid0, mid1, mid2, mid3, out_v,
    load_sem, ag_send, ag_recv, ex_send, ex_recv, store_sem,
):
    mids = (mid0, mid1, mid2, mid3)
    dp, fs, cx, core, y, z = place()
    sibling = (dp + 1 - 2 * core, fs)

    def at(dy, dz):
        return (dp, ((y + dy) % 4) * 4 + (z + dz) % 4)

    peers = [((dp + k) % NDP, fs) for k in range(1, NDP)]
    peers += [at(1, 0), at(3, 0), at(0, 1), at(0, 3)]
    load_x = pltpu.make_async_copy(x_hbm, x_v, load_sem.at[KVH])
    load_w = [
        pltpu.make_async_copy(
            w_hbm.at[core, :, pl.ds(h * HD, HD)], w_v.at[core, h, y, z], load_sem.at[h]
        )
        for h in range(KVH)
    ]
    for copy in load_w:
        copy.start()
    load_x.start()
    entry_barrier(peers)
    for copy in load_w:
        copy.wait()
    sends = Sends()

    def block(h, s, d1, d2, low, rows):
        dy, dz = (d1, d2) if s == 0 else (d2, d1)
        return w_v.at[core, h, (y + dy) % 4, (z + dz) % 4, pl.ds(s * HALF + low, rows), :]

    def ahead(s, axis, step):
        return at(step, 0) if (s == 0) == (axis == 1) else at(0, step)

    def pass_on(h, s, axis, step, ref, slot):
        sends.start(ref, ref, ag_send.at[h, s, slot], ag_recv.at[h, s, slot], ahead(s, axis, step))

    def landed(h, s, ref, slot):
        remote(ref, ref, ag_send.at[h, s, slot], ag_recv.at[h, s, slot], sibling).wait_recv()

    quarter = HALF // 2

    def both_ways(h, s, b):
        ref = block(h, s, b, 0, 0, HALF)
        pass_on(h, s, 2, 1, ref, 4 + 4 * b)
        pass_on(h, s, 2, 3, ref, 5 + 4 * b)

    def own(h):
        for s in range(2):
            ref = block(h, s, 0, 0, 0, HALF)
            pass_on(h, s, 1, 1, ref, 0)
            pass_on(h, s, 1, 3, ref, 1)
        for s in range(2):
            both_ways(h, s, 0)

    def near(h):
        for s in range(2):
            landed(h, s, block(h, s, 3, 0, 0, HALF), 0)
            pass_on(h, s, 1, 1, block(h, s, 3, 0, 0, quarter), 2)
            landed(h, s, block(h, s, 1, 0, 0, HALF), 1)
            pass_on(h, s, 1, 3, block(h, s, 1, 0, quarter, quarter), 3)
        for s in range(2):
            both_ways_from(h, s)

    def both_ways_from(h, s):
        for b in (3, 1):
            both_ways(h, s, b)

    def far(h):
        for s in range(2):
            landed(h, s, block(h, s, 2, 0, 0, quarter), 2)
            landed(h, s, block(h, s, 2, 0, quarter, quarter), 3)
            both_ways(h, s, 2)

    def relay(h, blocks):
        for b in blocks:
            for s in range(2):
                landed(h, s, block(h, s, b, 3, 0, HALF), 4 + 4 * b)
                pass_on(h, s, 2, 1, block(h, s, b, 3, 0, quarter), 6 + 4 * b)
                landed(h, s, block(h, s, b, 1, 0, HALF), 5 + 4 * b)
                pass_on(h, s, 2, 3, block(h, s, b, 1, quarter, quarter), 7 + 4 * b)

    def share(h):
        for b in (0, 3, 1, 2):
            for s in range(2):
                landed(h, s, block(h, s, b, 2, 0, quarter), 6 + 4 * b)
                landed(h, s, block(h, s, b, 2, quarter, quarter), 7 + 4 * b)
        sends.start(
            w_v.at[core, h], w_v.at[core, h], ex_send.at[h, 0, 0], ex_recv.at[h, 0, 0], sibling
        )

    stores = []

    def project(h):
        other = w_v.at[1 - core, h]
        remote(other, other, ex_send.at[h, 0, 0], ex_recv.at[h, 0, 0], sibling).wait_recv()
        for c in range(2):
            copy = pltpu.make_async_copy(w_v.at[c, h], wfull_hbm.at[c, h], store_sem.at[2 * h + c])
            copy.start()
            stores.append(copy)

        @pl.loop(0, 2)
        def _(part):
            rows = pl.ds(pl.multiple_of(part * 256, 256), 256)
            weights = jnp.concatenate(
                [w_v[0, h].reshape(D, HD), w_v[1, h].reshape(D, HD)], axis=1
            )
            both = jnp.dot(x_v[rows, :], weights, preferred_element_type=F32)
            raw = both[:, :HD]
            raw_ref[h, rows, :] = raw
            scale = lax.rsqrt(jnp.mean(raw * raw, axis=1, keepdims=True) + EPS)
            normed = raw * scale * gain_ref[...]
            rot = normed * cos_ref[rows, :] + swap_lanes(normed) * sin_ref[rows, :]
            tile_v[h, rows, :] = jnp.concatenate([rot, both[:, HD:]], axis=1).astype(BF)

        for k in range(1, NDP):
            to = (dp + k) % NDP
            sends.start(
                tile_v.at[h, pl.ds(to * PIECE, PIECE), :], mids[h].at[dp],
                ex_send.at[h, 0, k], ex_recv.at[h, 0, k], (to, fs),
            )
        mids[h][dp] = tile_v[h, pl.ds(pl.multiple_of(dp * PIECE, PIECE), PIECE), :]

    def forward(h):
        for k in range(1, NDP):
            ref = mids[h].at[(dp + NDP - k) % NDP]
            remote(ref, ref, ex_send.at[h, 0, k], ex_recv.at[h, 0, k], sibling).wait_recv()
        for k in range(NDP):
            to = (dp + k) % NDP
            out_v[h, k] = mids[h][pick_ref[to]]
            ref = kv_hbm.at[h, pl.ds(dp * PIECE, PIECE), :]
            if k == 0:
                copy = pltpu.make_async_copy(out_v.at[h, k], ref, store_sem.at[2 * KVH + h])
                copy.start()
                stores.append(copy)
            else:
                sends.start(
                    out_v.at[h, k], ref, ex_send.at[h, 1, k], ex_recv.at[h, 1, k], (to, fs)
                )

    def arrive(h):
        for k in range(1, NDP):
            ref = kv_hbm.at[h, pl.ds(((dp + NDP - k) % NDP) * PIECE, PIECE), :]
            remote(ref, ref, ex_send.at[h, 1, k], ex_recv.at[h, 1, k], sibling).wait_recv()

    def turn(h):
        if h == 0:
            load_x.wait()

        step = D // KVH

        @pl.loop(0, step // 256)
        def _(part):
            start = pl.multiple_of(h * step + part * 256, 256)
            xt_v[pl.ds(start, 256), :] = x_v[:, pl.ds(start, 256)].T

        copy = pltpu.make_async_copy(
            xt_v.at[pl.ds(h * step, step)], xt_hbm.at[pl.ds(h * step, step)],
            store_sem.at[3 * KVH + h],
        )
        copy.start()
        stores.append(copy)

    def relay_early(h):
        relay(h, (0, 3, 1))

    def relay_late(h):
        relay(h, (2,))

    def near_turn(h):
        near(h)
        turn(h)

    stages = [own, near_turn, far, relay_early, relay_late, share, project, forward, arrive]
    skewed(stages, KVH)
    sends.drain()
    for copy in stores:
        copy.wait()


def gather_call(x, weights, gain, cosine, sine, pick):
    any_spec = pl.BlockSpec(memory_space=pl.ANY)
    vmem_spec = pl.BlockSpec(memory_space=pltpu.VMEM)
    return pl.pallas_call(
        gather_kernel,
        out_shape=(
            jax.ShapeDtypeStruct((2, KVH, 4, 4, SHARD, HD), BF),
            jax.ShapeDtypeStruct((KVH, TILE, 2 * HD), BF),
            jax.ShapeDtypeStruct((KVH, TILE, HD), F32),
            jax.ShapeDtypeStruct((D, TILE), BF),
        ),
        in_specs=[any_spec, any_spec, vmem_spec, vmem_spec, vmem_spec,
                  pl.BlockSpec(memory_space=pltpu.SMEM)],
        out_specs=(any_spec, any_spec, vmem_spec, any_spec),
        scratch_shapes=[
            pltpu.VMEM((TILE, D), BF),
            pltpu.VMEM((2, KVH, 4, 4, SHARD, HD), BF),
            pltpu.VMEM((D, TILE), BF),
            pltpu.VMEM((KVH, TILE, 2 * HD), BF),
            *[pltpu.VMEM((NDP, PIECE, 2 * HD), BF)] * KVH,
            pltpu.VMEM((KVH, NDP, PIECE, 2 * HD), BF),
            pltpu.SemaphoreType.DMA((KVH + 1,)),
            pltpu.SemaphoreType.DMA((KVH, 2, 20)),
            pltpu.SemaphoreType.DMA((KVH, 2, 20)),
            pltpu.SemaphoreType.DMA((KVH, 2, NDP)),
            pltpu.SemaphoreType.DMA((KVH, 2, NDP)),
            pltpu.SemaphoreType.DMA((4 * KVH,)),
        ],
        compiler_params=pltpu.CompilerParams(
            collective_id=0, has_side_effects=True, vmem_limit_bytes=VMEM_LIMIT
        ),
        name="gather_project_send",
    )(x, weights, gain, cosine, sine, pick)


def attention_kernel(
    q_ref, og_ref, kv_ref, gain_ref, cos_ref, sin_ref, coef_ref,
    dq_ref, gkv_ref, gq_ref,
    kt_v, vt_v, va_v, acc_k, acc_v, acc_gain,
):
    step = pl.program_id(0)
    inner = step % GROUP

    @pl.when(step == 0)
    def _():
        acc_gain[...] = jnp.zeros_like(acc_gain)

    @pl.when(inner == 0)
    def _():
        keys, values = kv_ref[0, :, :HD], kv_ref[0, :, HD:]
        ones = jnp.ones((TILE, HD), BF)
        kt_v[...] = keys.T
        vt_v[:HD, :] = values.T
        vt_v[HD:, :] = jnp.ones((HD, TILE), BF)
        va_v[:, :HD] = values
        va_v[:, HD:] = ones
        acc_k[...] = jnp.zeros_like(acc_k)
        acc_v[...] = jnp.zeros_like(acc_v)

    half = HD // 2

    def swap(values):
        return jnp.concatenate([values[half:], values[:half]], axis=0)

    cosine, sine, gain = cos_ref[...], sin_ref[...], gain_ref[...]
    raw = q_ref[...].astype(F32).T
    scale = lax.rsqrt(jnp.mean(raw * raw, axis=0, keepdims=True) + EPS)
    unit = raw * scale
    normed = unit * gain
    rot = normed * cosine + swap(normed) * sine
    query = (rot * (math.log2(math.e) / math.sqrt(HD))).astype(BF)
    weighted = (og_ref[...].astype(F32).T * coef_ref[...]).astype(BF).astype(F32)

    contract_lanes = (((1,), (1,)), ((), ()))
    row = lax.broadcasted_iota(jnp.int32, (256, 256), 0)
    lane = lax.broadcasted_iota(jnp.int32, (256, 256), 1)
    causal = row <= lane
    sub = lax.broadcasted_iota(jnp.int32, (HD, 256), 0)
    grads = []
    for ib in range(2):
        cols = slice(ib * 256, ib * 256 + 256)
        seen = ib * 256 + 256
        qb = query[:, cols]
        scores = jnp.dot(kv_ref[0, :seen, :HD], qb, preferred_element_type=F32)
        weight = jnp.exp2(scores)
        last = jnp.where(causal, weight[ib * 256:], 0.0)
        weight = last if ib == 0 else jnp.concatenate([weight[:256], last], axis=0)
        low = weight.astype(BF)
        sums = jnp.dot(vt_v[:, :seen], low, preferred_element_type=F32)
        inverse = 1.0 / sums[HD:]
        attended = sums[:HD] * inverse
        scaled = (weighted[:, cols] * inverse).astype(BF)
        dotted = jnp.sum(scaled.astype(F32) * attended, axis=0, keepdims=True)
        high = dotted.astype(BF).astype(F32)
        rest = dotted - high
        tail = jnp.where(sub == 0, -high, jnp.where(sub == 1, -rest, 0.0)).astype(BF)
        grad_probs = jnp.dot(
            va_v[:seen, :], jnp.concatenate([scaled, tail], axis=0), preferred_element_type=F32
        )
        grad_scores = (weight * grad_probs).astype(BF)
        acc_v[:seen, :] += lax.dot_general(low, scaled, contract_lanes, preferred_element_type=F32)
        acc_k[:seen, :] += lax.dot_general(
            grad_scores, qb, contract_lanes, preferred_element_type=F32
        )
        grads.append(jnp.dot(kt_v[:, :seen], grad_scores, preferred_element_type=F32))
    grad_rot = jnp.concatenate(grads, axis=1) * (1.0 / math.sqrt(HD))
    grad_normed = grad_rot * cosine - swap(grad_rot) * sine
    terms = grad_normed * unit
    acc_gain[...] += terms[:, :128] + terms[:, 128:256] + terms[:, 256:384] + terms[:, 384:]
    mean = jnp.mean(terms * gain, axis=0, keepdims=True)
    dq_ref[...] = (scale * (grad_normed * gain - unit * mean)).T.astype(BF)

    @pl.when(inner == GROUP - 1)
    def _():
        gkv_ref[0, :, :HD] = (acc_k[...] * math.log(2.0)).astype(BF)
        gkv_ref[0, :, HD:] = acc_v[...].astype(BF)

    @pl.when(step == QH - 1)
    def _():
        gq_ref[...] = jnp.sum(acc_gain[...].T, axis=0, keepdims=True)


def attention_call(queries, out_grad, kv, gain, cosine, sine, coef):
    head_spec = pl.BlockSpec((TILE, HD), lambda n: (0, n))
    kv_spec = pl.BlockSpec((1, TILE, 2 * HD), lambda n: (n // GROUP, 0, 0))
    whole = lambda shape: pl.BlockSpec(shape, lambda n: (0, 0))
    return pl.pallas_call(
        attention_kernel,
        grid=(QH,),
        out_shape=(
            jax.ShapeDtypeStruct((TILE, QH * HD), BF),
            jax.ShapeDtypeStruct((KVH, TILE, 2 * HD), BF),
            jax.ShapeDtypeStruct((1, HD), F32),
        ),
        in_specs=[head_spec, head_spec, kv_spec, whole((HD, TILE)), whole((HD, TILE)),
                  whole((HD, TILE)), whole((1, TILE))],
        out_specs=(head_spec, kv_spec, whole((1, HD))),
        scratch_shapes=[
            pltpu.VMEM((HD, TILE), BF),
            pltpu.VMEM((2 * HD, TILE), BF),
            pltpu.VMEM((TILE, 2 * HD), BF),
            pltpu.VMEM((TILE, HD), F32),
            pltpu.VMEM((TILE, HD), F32),
            pltpu.VMEM((HD, HD), F32),
        ],
        compiler_params=pltpu.CompilerParams(vmem_limit_bytes=VMEM_LIMIT),
        name="attention_both_ways",
    )(queries, out_grad, kv, gain, cosine, sine, coef)


def reduce_kernel(
    gkv_hbm, xt_hbm, raw_ref, gq_ref, gain_ref, cos_ref, sin_ref, pick_ref,
    g_ref, outk_ref, outv_ref, gain_out,
    xt_v, mid0, mid1, mid2, mid3, pass_v, back_v, dw_v, pair_v, r1_v, r2_v, q_v, r4_v, r5_v, f_v, r7_v, full_v,
    gain_v, gain_r,
    load_sem, ex_send, ex_recv, rs_send, rs_recv, x_send, x_recv, gn_send, gn_recv,
):
    mids = (mid0, mid1, mid2, mid3)
    dp, fs, cx, core, y, z = place()
    sibling = (dp + 1 - 2 * core, fs)

    def at(dy, dz):
        return (dp, ((y + dy) % 4) * 4 + (z + dz) % 4)

    peers = [((dp + k) % NDP, fs) for k in range(1, NDP)]
    peers += [at(k, 0) for k in range(1, 4)] + [at(0, k) for k in range(1, 4)]
    load_x = pltpu.make_async_copy(xt_hbm, xt_v, load_sem.at[0])
    load_x.start()
    own_copies = []
    for h in range(KVH):
        copy = pltpu.make_async_copy(
            gkv_hbm.at[h, pl.ds(dp * PIECE, PIECE), :], mids[h].at[dp], load_sem.at[1 + h]
        )
        copy.start()
        own_copies.append(copy)
    entry_barrier(peers)
    sends = Sends()

    def spread(h):
        for k in range(1, NDP):
            to = (dp + k) % NDP
            sends.start(
                gkv_hbm.at[h, pl.ds(to * PIECE, PIECE), :], mids[h].at[dp],
                ex_send.at[h, 0, k], ex_recv.at[h, 0, k], (to, fs),
            )

    def forward(h):
        own_copies[h].wait()
        for k in range(1, NDP):
            ref = mids[h].at[(dp + NDP - k) % NDP]
            remote(ref, ref, ex_send.at[h, 0, k], ex_recv.at[h, 0, k], sibling).wait_recv()
        for k in range(NDP):
            to = (dp + k) % NDP
            if k == 0:
                back_v[h, dp] = mids[h][pick_ref[to]]
            else:
                pass_v[h, k] = mids[h][pick_ref[to]]
                sends.start(
                    pass_v.at[h, k], back_v.at[h, dp],
                    ex_send.at[h, 1, k], ex_recv.at[h, 1, k], (to, fs),
                )

    gain_parts = []

    def multiply(h):
        if h == 0:
            load_x.wait()
        for k in range(1, NDP):
            ref = back_v.at[h, (dp + NDP - k) % NDP]
            remote(ref, ref, ex_send.at[h, 1, k], ex_recv.at[h, 1, k], sibling).wait_recv()
        grads = back_v[h].reshape(TILE, 2 * HD)
        grad_rot = grads[:, :HD].astype(F32)
        raw = raw_ref[h]
        scale = lax.rsqrt(jnp.mean(raw * raw, axis=1, keepdims=True) + EPS)
        unit = raw * scale
        normed = grad_rot * cos_ref[...] - swap_lanes(grad_rot) * sin_ref[...]
        terms = normed * unit
        gain_parts.append(jnp.sum(terms, axis=0, keepdims=True))
        gained = normed * gain_ref[...]
        mean = jnp.mean(gained * unit, axis=1, keepdims=True)
        g_ref[h, :, :HD] = (scale * (gained - unit * mean)).astype(BF)
        g_ref[h, :, HD:] = grads[:, HD:]

        @pl.loop(0, 16)
        def _(shard):
            sy, sz = shard // 4, shard % 4
            start = pl.multiple_of(shard * SHARD, SHARD)
            part = jnp.dot(xt_v[pl.ds(start, SHARD), :], g_ref[h], preferred_element_type=F32)
            part = part.astype(BF)
            for c in range(2):
                dw_v[h, c, 0, sz, sy] = part[:HALF, c * HD:(c + 1) * HD]
                dw_v[h, c, 1, sy, sz] = part[HALF:, c * HD:(c + 1) * HD]

        for s in range(2):
            sends.start(
                dw_v.at[h, 1 - core, s], pair_v.at[h, s],
                rs_send.at[h, s, 0], rs_recv.at[h, s, 0], sibling,
            )

    def me(s, axis):
        return z if (s == 0) == (axis == 1) else y

    def ahead(s, axis, step):
        return at(0, step) if (s == 0) == (axis == 1) else at(step, 0)

    def send(h, s, slot, src, dst, axis, step):
        sends.start(src, dst, rs_send.at[h, s, slot], rs_recv.at[h, s, slot], ahead(s, axis, step))

    def landed(h, s, slot, ref):
        remote(ref, ref, rs_send.at[h, s, slot], rs_recv.at[h, s, slot], sibling).wait_recv()

    def add(ref, *others):
        total = ref[...].astype(F32)
        for other in others:
            total = total + other[...].astype(F32)
        ref[...] = total.astype(BF)

    def pair(h):
        for s in range(2):
            landed(h, s, 0, pair_v.at[h, s])
            mine = dw_v.at[h, core, s]
            far = (me(s, 1) + 2) % 4
            add(mine.at[far], pair_v.at[h, s, far])
            send(h, s, 1, mine.at[far, 0:2], r1_v.at[h, s, 0], 1, 1)
            send(h, s, 2, mine.at[far, 2:4], r1_v.at[h, s, 1], 1, 3)
        for s in range(2):
            mine = dw_v.at[h, core, s]
            for step in (1, 3, 0):
                index = (me(s, 1) + step) % 4
                add(mine.at[index], pair_v.at[h, s, index])

    def near(h):
        for s in range(2):
            mine = dw_v.at[h, core, s]
            up, down = (me(s, 1) + 1) % 4, (me(s, 1) + 3) % 4
            landed(h, s, 1, r1_v.at[h, s, 0])
            add(mine.at[up, 0:2], r1_v.at[h, s, 0])
            send(h, s, 3, mine.at[up], r2_v.at[h, s, 0], 1, 1)
            landed(h, s, 2, r1_v.at[h, s, 1])
            add(mine.at[down, 2:4], r1_v.at[h, s, 1])
            send(h, s, 4, mine.at[down], r2_v.at[h, s, 1], 1, 3)

    quarter = HALF // 2

    def cross(h):
        for s in range(2):
            landed(h, s, 3, r2_v.at[h, s, 0])
            landed(h, s, 4, r2_v.at[h, s, 1])
            own = dw_v[h, core, s, me(s, 1)].astype(F32)
            q_v[h, s] = (own + r2_v[h, s, 0].astype(F32) + r2_v[h, s, 1].astype(F32)).astype(BF)
            far = (me(s, 2) + 2) % 4
            send(h, s, 5, q_v.at[h, s, far, 0:quarter], r4_v.at[h, s, 0], 2, 1)
            send(h, s, 6, q_v.at[h, s, far, quarter:HALF], r4_v.at[h, s, 1], 2, 3)

    def near_cross(h):
        for s in range(2):
            up, down = (me(s, 2) + 1) % 4, (me(s, 2) + 3) % 4
            landed(h, s, 5, r4_v.at[h, s, 0])
            add(q_v.at[h, s, up, 0:quarter], r4_v.at[h, s, 0])
            send(h, s, 7, q_v.at[h, s, up], r5_v.at[h, s, 0], 2, 1)
            landed(h, s, 6, r4_v.at[h, s, 1])
            add(q_v.at[h, s, down, quarter:HALF], r4_v.at[h, s, 1])
            send(h, s, 8, q_v.at[h, s, down], r5_v.at[h, s, 1], 2, 3)

    def along_x(h):
        for s in range(2):
            landed(h, s, 7, r5_v.at[h, s, 0])
            landed(h, s, 8, r5_v.at[h, s, 1])
            own = q_v[h, s, me(s, 2)].astype(F32)
            f_v[h, s * HALF:(s + 1) * HALF] = (
                own + r5_v[h, s, 0].astype(F32) + r5_v[h, s, 1].astype(F32)
            ).astype(BF)
        for k in range(1, 4):
            to = (cx + k) % 4
            sends.start(
                f_v.at[h, pl.ds(to * 80, 80), :], r7_v.at[h, k - 1],
                x_send.at[h, k - 1], x_recv.at[h, k - 1], (to * 2 + core, fs),
            )

    def spread_x(h):
        for k in range(1, 4):
            ref = r7_v.at[h, k - 1]
            remote(ref, ref, x_send.at[h, k - 1], x_recv.at[h, k - 1], sibling).wait_recv()
        rows = pl.ds(pl.multiple_of(cx * 80, 80), 80)
        total = f_v[h, rows, :].astype(F32)
        for k in range(3):
            total = total + r7_v[h, k].astype(F32)
        full_v[h, core, rows, :] = total.astype(BF)
        for k in range(1, NDP):
            ref = full_v.at[h, core, rows, :]
            sends.start(ref, ref, x_send.at[h, 2 + k], x_recv.at[h, 2 + k], ((dp + k) % NDP, fs))

    def finish(h):
        for k in range(1, NDP):
            source = (dp + NDP - k) % NDP
            ref = full_v.at[h, source % 2, pl.ds((source // 2) * 80, 80), :]
            remote(ref, ref, x_send.at[h, 2 + k], x_recv.at[h, 2 + k], sibling).wait_recv()
        outk_ref[:, h * HD:(h + 1) * HD] = full_v[h, 0].astype(F32)
        outv_ref[:, h * HD:(h + 1) * HD] = full_v[h, 1].astype(F32)

    groups = [
        (0, [((dp + k) % NDP, fs) for k in range(1, NDP)]),
        (7, [at(k, 0) for k in range(1, 4)]),
        (10, [at(0, k) for k in range(1, 4)]),
    ]

    def gains_out(stage):
        base, targets = groups[stage]
        for k, target in enumerate(targets):
            sends.start(
                gain_v.at[stage], gain_r.at[base + k], gn_send.at[base + k], gn_recv.at[base + k],
                target,
            )

    def gains_in(stage):
        base, targets = groups[stage]
        total = gain_v[stage]
        for k in range(len(targets)):
            ref = gain_r.at[base + k]
            remote(ref, ref, gn_send.at[base + k], gn_recv.at[base + k], sibling).wait_recv()
            total = total + gain_r[base + k]
        gain_v[stage + 1] = total

    def gains(stage):
        if stage == 0:
            row = lax.broadcasted_iota(jnp.int32, (8, HD), 0)
            keys = gain_parts[0] + gain_parts[1] + gain_parts[2] + gain_parts[3]
            gain_v[0] = jnp.where(row == 0, gq_ref[...], jnp.where(row == 1, keys, 0.0))
        else:
            gains_in(stage - 1)
        if stage < 3:
            gains_out(stage)
        else:
            gain_out[...] = gain_v[3]

    def then_gains(stage_function, stage):
        def both(h):
            stage_function(h)
            if h == KVH - 1:
                gains(stage)

        return both

    stages = [
        spread, forward, then_gains(multiply, 0), pair, then_gains(near, 1), then_gains(cross, 2),
        then_gains(near_cross, 3), along_x, spread_x, finish,
    ]
    skewed(stages, KVH)
    sends.drain()


def reduce_call(gkv, xt, raw, gq, gain, cosine, sine, pick):
    any_spec = pl.BlockSpec(memory_space=pl.ANY)
    vmem_spec = pl.BlockSpec(memory_space=pltpu.VMEM)
    return pl.pallas_call(
        reduce_kernel,
        out_shape=(
            jax.ShapeDtypeStruct((KVH, TILE, 2 * HD), BF),
            jax.ShapeDtypeStruct((SHARD, KVH * HD), F32),
            jax.ShapeDtypeStruct((SHARD, KVH * HD), F32),
            jax.ShapeDtypeStruct((8, HD), F32),
        ),
        in_specs=[any_spec, any_spec] + [vmem_spec] * 5 + [pl.BlockSpec(memory_space=pltpu.SMEM)],
        out_specs=(vmem_spec,) * 4,
        scratch_shapes=[
            pltpu.VMEM((D, TILE), BF),
            *[pltpu.VMEM((NDP, PIECE, 2 * HD), BF)] * KVH,
            pltpu.VMEM((KVH, NDP, PIECE, 2 * HD), BF),
            pltpu.VMEM((KVH, NDP, PIECE, 2 * HD), BF),
            pltpu.VMEM((KVH, 2, 2, 4, 4, HALF, HD), BF),
            pltpu.VMEM((KVH, 2, 4, 4, HALF, HD), BF),
            pltpu.VMEM((KVH, 2, 2, 2, HALF, HD), BF),
            pltpu.VMEM((KVH, 2, 2, 4, HALF, HD), BF),
            pltpu.VMEM((KVH, 2, 4, HALF, HD), BF),
            pltpu.VMEM((KVH, 2, 2, HALF // 2, HD), BF),
            pltpu.VMEM((KVH, 2, 2, HALF, HD), BF),
            pltpu.VMEM((KVH, SHARD, HD), BF),
            pltpu.VMEM((KVH, 3, 80, HD), BF),
            pltpu.VMEM((KVH, 2, SHARD, HD), BF),
            pltpu.VMEM((4, 8, HD), F32),
            pltpu.VMEM((13, 8, HD), F32),
            pltpu.SemaphoreType.DMA((KVH + 1,)),
            pltpu.SemaphoreType.DMA((KVH, 2, NDP)),
            pltpu.SemaphoreType.DMA((KVH, 2, NDP)),
            pltpu.SemaphoreType.DMA((KVH, 2, 9)),
            pltpu.SemaphoreType.DMA((KVH, 2, 9)),
            pltpu.SemaphoreType.DMA((KVH, 10)),
            pltpu.SemaphoreType.DMA((KVH, 10)),
            pltpu.SemaphoreType.DMA((13,)),
            pltpu.SemaphoreType.DMA((13,)),
        ],
        compiler_params=pltpu.CompilerParams(
            collective_id=1, has_side_effects=True, vmem_limit_bytes=VMEM_LIMIT
        ),
        name="return_multiply_reduce",
    )(gkv, xt, raw, gq, gain, cosine, sine, pick)


def hidden_kernel(g_ref, w_ref, out_ref):
    grads = jnp.concatenate(
        [g_ref[h, :, c * HD:(c + 1) * HD] for h in range(KVH) for c in range(2)], axis=1
    )
    weights = jnp.concatenate([w_ref[c, h] for h in range(KVH) for c in range(2)], axis=1)
    out_ref[...] = lax.dot_general(
        grads, weights, (((1,), (1,)), ((), ())), preferred_element_type=F32
    ).astype(BF)


def hidden_call(g, weights):
    block = 512
    return pl.pallas_call(
        hidden_kernel,
        grid=(D // block,),
        out_shape=jax.ShapeDtypeStruct((TILE, D), BF),
        in_specs=[
            pl.BlockSpec((KVH, TILE, 2 * HD), lambda n: (0, 0, 0)),
            pl.BlockSpec((2, KVH, block, HD), lambda n: (0, 0, n, 0)),
        ],
        out_specs=pl.BlockSpec((TILE, block), lambda n: (0, n)),
        compiler_params=pltpu.CompilerParams(vmem_limit_bytes=VMEM_LIMIT),
        name="hidden_gradient",
    )(g, weights)


def per_device(
    rollout_hidden, key_weight, value_weight, key_gain, query_gain, queries, out_grad, rewards,
    response_lengths, rollout_owner, train_shard, pack_offsets,
):
    del pack_offsets
    dp = lax.axis_index("dp")
    lengths, owners, trainers = response_lengths[0], rollout_owner[0], train_shard[0]
    index = jnp.arange(NDP, dtype=jnp.int32)
    by_trainer = (trainers[None, :] == index[:, None]).astype(jnp.int32)
    by_owner = (owners[None, :] == index[:, None]).astype(jnp.int32)
    owner_of = jnp.sum(by_trainer * owners[None, :], axis=1)
    trainer_of = jnp.sum(by_owner * trainers[None, :], axis=1)
    grouped = rewards[0].reshape(-1, GSIZE)
    advantage = (grouped - jnp.mean(grouped, axis=-1, keepdims=True)).reshape(-1)
    mine = trainers == dp
    length = jnp.sum(jnp.where(mine, lengths, 0))
    factor = jnp.sum(jnp.where(mine, advantage, 0.0))
    coef = jnp.where(jnp.arange(TILE) < length, factor, 0.0).reshape(1, TILE)

    cosine, sine = rope_arrays()
    key_gain_row = key_gain.reshape(1, HD)
    query_gain_wide = jnp.broadcast_to(query_gain[:, None], (HD, TILE))
    weights = jnp.stack([key_weight, value_weight])
    full, kv, raw, xt = gather_call(
        rollout_hidden, weights, key_gain_row, cosine, sine, owner_of
    )
    d_queries, gkv, gq = attention_call(
        queries, out_grad, kv, query_gain_wide,
        np.ascontiguousarray(cosine.T), np.ascontiguousarray(sine.T), coef,
    )
    g, grad_key_weight, grad_value_weight, gains = reduce_call(
        gkv, xt, raw, gq, key_gain_row, cosine, sine, trainer_of
    )
    d_hidden = hidden_call(g, full.reshape(2, KVH, D, HD))
    return d_hidden, d_queries, grad_key_weight, grad_value_weight, gains[0], gains[1]


def solution(mesh):
    rows, split = P(("dp", "fsdp"), None), P("fsdp", None)
    return jax.shard_map(
        per_device,
        mesh=mesh,
        in_specs=(rows, split, split, P(), P(), rows, rows, split, split, split, split, split),
        out_specs=(rows, rows, split, split, P(), P()),
        check_vma=False,
    )
```

```python
import functools
import math

import jax
import jax.numpy as jnp
import numpy as np
from jax import lax
from jax.experimental import pallas as pl
from jax.experimental.pallas import tpu as pltpu
from jax.sharding import PartitionSpec as P

MESH = pl.DeviceIdType.MESH
BF, F32 = jnp.bfloat16, jnp.float32
HD = 128
GSIZE = 4
TILE = 512
D = 5120
KVH = 4
QH = 32
GROUP = QH // KVH
NDP = 8
SHARD = 320
HALF = SHARD // 2
PIECE = TILE // NDP
EPS = 1e-06
VMEM_LIMIT = 60 * 1024 * 1024


def rope_arrays():
    half = HD // 2
    frequency = 1000000.0 ** (-np.arange(half, dtype=np.float64) / half)
    angles = np.arange(TILE, dtype=np.float64)[:, None] * frequency[None, :]
    cosine, sine = np.cos(angles), np.sin(angles)
    return (
        np.concatenate([cosine, cosine], axis=1).astype(np.float32),
        np.concatenate([-sine, sine], axis=1).astype(np.float32),
    )


def place():
    dp, fs = lax.axis_index("dp"), lax.axis_index("fsdp")
    return dp, fs, dp // 2, dp % 2, fs // 4, fs % 4


def remote(src, dst, send, recv, device):
    return pltpu.make_async_remote_copy(
        src_ref=src, dst_ref=dst, send_sem=send, recv_sem=recv, device_id=device, device_id_type=MESH
    )


def entry_barrier(peers):
    barrier = pltpu.get_barrier_semaphore()
    for peer in peers:
        pl.semaphore_signal(barrier, inc=1, device_id=peer, device_id_type=MESH)
    pl.semaphore_wait(barrier, len(peers))


def match(labels_ref, values_ref, label):
    found = jnp.int32(0)
    for r in range(NDP):
        found = jnp.where(labels_ref[0, r] == label, values_ref[0, r], found)
    return found


def swap_lanes(values):
    return pltpu.roll(values, HD // 2, axis=1)


class Sends:
    def __init__(self):
        self.pending = []

    def start(self, *args):
        copy = remote(*args)
        copy.start()
        self.pending.append(copy)

    def drain(self):
        for copy in self.pending:
            copy.wait_send()
        self.pending = []


def skewed(stages, chunks, beside=()):
    for tick in range(len(stages) + chunks - 1):
        for chunk in reversed(range(chunks)):
            if 0 <= tick - chunk < len(stages):
                stages[tick - chunk](chunk)
        for when, work in beside:
            if when == tick:
                work()


def gather_kernel(
    x_hbm, kw_hbm, vw_hbm, gain_ref, cos_ref, sin_ref, owner_ref, trainer_ref,
    wt_hbm, kv_hbm, raw_ref, xt_hbm,
    x_v, w_v, wt_v, xt_v, tile_v, mid0, mid1, mid2, mid3, out_v,
    load_sem, ag_send, ag_recv, ex_send, ex_recv, store_sem,
):
    mids = (mid0, mid1, mid2, mid3)
    dp, fs, cx, core, y, z = place()
    sibling = (dp + 1 - 2 * core, fs)

    def at(dy, dz):
        return (dp, ((y + dy) % 4) * 4 + (z + dz) % 4)

    peers = [((dp + k) % NDP, fs) for k in range(1, NDP)]
    peers += [at(1, 0), at(3, 0), at(0, 1), at(0, 3)]
    load_x = pltpu.make_async_copy(x_hbm, x_v, load_sem.at[KVH])

    def load_w(h, source):
        return pltpu.make_async_copy(
            source.at[:, pl.ds(h * HD, HD)], w_v.at[core, h, y, z], load_sem.at[h]
        )

    for h in range(KVH):
        @pl.when(core == 0)
        def _():
            load_w(h, kw_hbm).start()

        @pl.when(core == 1)
        def _():
            load_w(h, vw_hbm).start()

    load_x.start()
    entry_barrier(peers)
    for h in range(KVH):
        load_w(h, kw_hbm).wait()
    sends = Sends()

    def block(h, s, d1, d2, low, rows):
        dy, dz = (d1, d2) if s == 0 else (d2, d1)
        return w_v.at[core, h, (y + dy) % 4, (z + dz) % 4, pl.ds(s * HALF + low, rows), :]

    def ahead(s, axis, step):
        return at(step, 0) if (s == 0) == (axis == 1) else at(0, step)

    def pass_on(h, s, axis, step, ref, slot):
        sends.start(ref, ref, ag_send.at[h, s, slot], ag_recv.at[h, s, slot], ahead(s, axis, step))

    def landed(h, s, ref, slot):
        remote(ref, ref, ag_send.at[h, s, slot], ag_recv.at[h, s, slot], sibling).wait_recv()

    quarter = HALF // 2

    def both_ways(h, s, b):
        ref = block(h, s, b, 0, 0, HALF)
        pass_on(h, s, 2, 1, ref, 4 + 4 * b)
        pass_on(h, s, 2, 3, ref, 5 + 4 * b)

    def own(h):
        for s in range(2):
            ref = block(h, s, 0, 0, 0, HALF)
            pass_on(h, s, 1, 1, ref, 0)
            pass_on(h, s, 1, 3, ref, 1)
        for s in range(2):
            both_ways(h, s, 0)

    def near(h):
        for s in range(2):
            landed(h, s, block(h, s, 3, 0, 0, HALF), 0)
            pass_on(h, s, 1, 1, block(h, s, 3, 0, 0, quarter), 2)
            landed(h, s, block(h, s, 1, 0, 0, HALF), 1)
            pass_on(h, s, 1, 3, block(h, s, 1, 0, quarter, quarter), 3)
        for s in range(2):
            both_ways_from(h, s)

    def both_ways_from(h, s):
        for b in (3, 1):
            both_ways(h, s, b)

    def far(h):
        for s in range(2):
            landed(h, s, block(h, s, 2, 0, 0, quarter), 2)
            landed(h, s, block(h, s, 2, 0, quarter, quarter), 3)
            both_ways(h, s, 2)

    def relay(h, blocks):
        for b in blocks:
            for s in range(2):
                landed(h, s, block(h, s, b, 3, 0, HALF), 4 + 4 * b)
                pass_on(h, s, 2, 1, block(h, s, b, 3, 0, quarter), 6 + 4 * b)
                landed(h, s, block(h, s, b, 1, 0, HALF), 5 + 4 * b)
                pass_on(h, s, 2, 3, block(h, s, b, 1, quarter, quarter), 7 + 4 * b)

    def share(h):
        for b in (0, 3, 1, 2):
            for s in range(2):
                landed(h, s, block(h, s, b, 2, 0, quarter), 6 + 4 * b)
                landed(h, s, block(h, s, b, 2, quarter, quarter), 7 + 4 * b)
        sends.start(
            w_v.at[core, h], w_v.at[core, h], ex_send.at[h, 0, 0], ex_recv.at[h, 0, 0], sibling
        )

    stores = []

    def project(h):
        other = w_v.at[1 - core, h]
        remote(other, other, ex_send.at[h, 0, 0], ex_recv.at[h, 0, 0], sibling).wait_recv()
        @pl.loop(0, 2)
        def _(part):
            rows = pl.ds(pl.multiple_of(part * 256, 256), 256)
            weights = jnp.concatenate(
                [w_v[0, h].reshape(D, HD), w_v[1, h].reshape(D, HD)], axis=1
            )
            both = jnp.dot(x_v[rows, :], weights, preferred_element_type=F32)
            raw = both[:, :HD]
            raw_ref[h, rows, :] = raw
            scale = lax.rsqrt(jnp.mean(raw * raw, axis=1, keepdims=True) + EPS)
            normed = raw * scale * gain_ref[...]
            rot = normed * cos_ref[rows, :] + swap_lanes(normed) * sin_ref[rows, :]
            tile_v[h, rows, :] = jnp.concatenate([rot, both[:, HD:]], axis=1).astype(BF)

        for k in range(1, NDP):
            to = (dp + k) % NDP
            sends.start(
                tile_v.at[h, pl.ds(to * PIECE, PIECE), :], mids[h].at[dp],
                ex_send.at[h, 0, k], ex_recv.at[h, 0, k], (to, fs),
            )
        mids[h][dp] = tile_v[h, pl.ds(pl.multiple_of(dp * PIECE, PIECE), PIECE), :]

        turn_weights(h)

    def turn_weights(h):
        @pl.loop(0, 4)
        def _(row):
            start = pl.multiple_of(row * 4 * SHARD, 4 * SHARD)
            for c in range(2):
                wt_v[2 * h + c, :, pl.ds(start, 4 * SHARD)] = w_v[c, h, row].reshape(4 * SHARD, HD).T

        copy = pltpu.make_async_copy(
            wt_v.at[pl.ds(2 * h, 2)], wt_hbm.at[pl.ds(2 * h, 2)], store_sem.at[h]
        )
        copy.start()
        stores.append(copy)

    def forward(h):
        for k in range(1, NDP):
            ref = mids[h].at[(dp + NDP - k) % NDP]
            remote(ref, ref, ex_send.at[h, 0, k], ex_recv.at[h, 0, k], sibling).wait_recv()
        for k in range(NDP):
            to = (dp + k) % NDP
            out_v[h, k] = mids[h][match(trainer_ref, owner_ref, to)]
            ref = kv_hbm.at[h, pl.ds(dp * PIECE, PIECE), :]
            if k == 0:
                copy = pltpu.make_async_copy(out_v.at[h, k], ref, store_sem.at[2 * KVH + h])
                copy.start()
                stores.append(copy)
            else:
                sends.start(
                    out_v.at[h, k], ref, ex_send.at[h, 1, k], ex_recv.at[h, 1, k], (to, fs)
                )

    def arrive(h):
        for k in range(1, NDP):
            ref = kv_hbm.at[h, pl.ds(((dp + NDP - k) % NDP) * PIECE, PIECE), :]
            remote(ref, ref, ex_send.at[h, 1, k], ex_recv.at[h, 1, k], sibling).wait_recv()

    def turn(h):
        if h == 0:
            load_x.wait()

        step = D // KVH
        xt_v[h * step:(h + 1) * step, :] = x_v[:, h * step:(h + 1) * step].T

        copy = pltpu.make_async_copy(
            xt_v.at[pl.ds(h * step, step)], xt_hbm.at[pl.ds(h * step, step)],
            store_sem.at[3 * KVH + h],
        )
        copy.start()
        stores.append(copy)

    def relay_early(h):
        relay(h, (0, 3, 1))

    def relay_late(h):
        relay(h, (2,))

    stages = [own, near, far, relay_early, relay_late, share, project, forward, arrive]
    skewed(stages, KVH, [(1 + h, functools.partial(turn, h)) for h in range(KVH)])
    sends.drain()
    for copy in stores:
        copy.wait()


def gather_call(x, key_weight, value_weight, gain, cosine, sine, owners, trainers):
    any_spec = pl.BlockSpec(memory_space=pl.ANY)
    vmem_spec = pl.BlockSpec(memory_space=pltpu.VMEM)
    return pl.pallas_call(
        gather_kernel,
        out_shape=(
            jax.ShapeDtypeStruct((2 * KVH, HD, D), BF),
            jax.ShapeDtypeStruct((KVH, TILE, 2 * HD), BF),
            jax.ShapeDtypeStruct((KVH, TILE, HD), F32),
            jax.ShapeDtypeStruct((D, TILE), BF),
        ),
        in_specs=[any_spec] * 3 + [vmem_spec] * 3 + [pl.BlockSpec(memory_space=pltpu.SMEM)] * 2,
        out_specs=(any_spec, any_spec, vmem_spec, any_spec),
        scratch_shapes=[
            pltpu.VMEM((TILE, D), BF),
            pltpu.VMEM((2, KVH, 4, 4, SHARD, HD), BF),
            pltpu.VMEM((2 * KVH, HD, D), BF),
            pltpu.VMEM((D, TILE), BF),
            pltpu.VMEM((KVH, TILE, 2 * HD), BF),
            *[pltpu.VMEM((NDP, PIECE, 2 * HD), BF)] * KVH,
            pltpu.VMEM((KVH, NDP, PIECE, 2 * HD), BF),
            pltpu.SemaphoreType.DMA((KVH + 1,)),
            pltpu.SemaphoreType.DMA((KVH, 2, 20)),
            pltpu.SemaphoreType.DMA((KVH, 2, 20)),
            pltpu.SemaphoreType.DMA((KVH, 2, NDP)),
            pltpu.SemaphoreType.DMA((KVH, 2, NDP)),
            pltpu.SemaphoreType.DMA((4 * KVH,)),
        ],
        compiler_params=pltpu.CompilerParams(
            collective_id=0, has_side_effects=True, vmem_limit_bytes=VMEM_LIMIT
        ),
        name="gather_project_send",
    )(x, key_weight, value_weight, gain, cosine, sine, owners, trainers)


HEADS = 4
QUADS = QH // HEADS


def reduce_kernel(
    rewards_ref, length_ref, owner_ref, trainer_ref,
    q_hbm, og_hbm, kv_hbm, xt_hbm, wt_hbm, raw_ref, qgain_ref, gain_ref, cos_ref, sin_ref,
    cost_ref, sint_ref,
    hidden_hbm, dq_hbm, outk_ref, outv_ref, gq_out, gk_out,
    q_in, og_in, dq_v, kv_v, gkv_v, kt_v, vt_v, acc_k, acc_v, acc_gain, wide_gain, coef_v,
    xt_v, wt_v, g_v, hidden_v, mid0, mid1, mid2, mid3, pass_v, back_v, dw_v, pair_v, r1_v, r2_v, q_v, f_v, r7_v, full_v,
    gain_v, gain_r,
    load_sem, head_sem, ex_send, ex_recv, rs_send, rs_recv, x_send, x_recv, gn_send, gn_recv,
):
    mids = (mid0, mid1, mid2, mid3)
    dp, fs, cx, core, y, z = place()
    sibling = (dp + 1 - 2 * core, fs)

    def at(dy, dz):
        return (dp, ((y + dy) % 4) * 4 + (z + dz) % 4)

    peers = [((dp + k) % NDP, fs) for k in range(1, NDP)]
    peers += [at(k, 0) for k in range(1, 4)] + [at(0, k) for k in range(1, 4)]
    load_kv = [
        pltpu.make_async_copy(kv_hbm.at[h], kv_v.at[h], load_sem.at[1 + h]) for h in range(KVH)
    ]
    load_x = pltpu.make_async_copy(xt_hbm, xt_v, load_sem.at[0])
    load_w = pltpu.make_async_copy(wt_hbm, wt_v, load_sem.at[KVH + 1])
    width = HEADS * HD

    def load_heads(quad):
        columns, slot = pl.ds(quad * width, width), quad % 2
        return (
            pltpu.make_async_copy(q_hbm.at[:, columns], q_in.at[slot], head_sem.at[0, slot]),
            pltpu.make_async_copy(og_hbm.at[:, columns], og_in.at[slot], head_sem.at[1, slot]),
        )

    def store_heads(quad):
        columns, slot = pl.ds(quad * width, width), quad % 2
        return pltpu.make_async_copy(dq_v.at[slot], dq_hbm.at[:, columns], head_sem.at[2, slot])

    load_kv[0].start()
    for copy in load_heads(0):
        copy.start()
    for copy in load_kv[1:]:
        copy.start()
    load_x.start()
    load_w.start()
    entry_barrier(peers)
    sends = Sends()

    acc_gain[...] = jnp.zeros_like(acc_gain)
    column = jnp.broadcast_to(qgain_ref[...], (HD, HD)).T
    wide_gain[...] = jnp.concatenate([column] * (TILE // HD), axis=1)
    length, factor = jnp.int32(0), jnp.float32(0.0)
    for r in range(NDP):
        group = (r // GSIZE) * GSIZE
        total = rewards_ref[0, group]
        for member in range(1, GSIZE):
            total = total + rewards_ref[0, group + member]
        mine = trainer_ref[0, r] == dp
        length = jnp.where(mine, length_ref[0, r], length)
        factor = jnp.where(mine, rewards_ref[0, r] - total * (1.0 / GSIZE), factor)
    position = lax.broadcasted_iota(jnp.int32, (1, TILE), 1)
    coef_v[...] = jnp.where(position < length, factor, 0.0)
    half = HD // 2

    def swap(values):
        return jnp.concatenate([values[half:], values[:half]], axis=0)

    contract_lanes = (((1,), (1,)), ((), ()))

    def attend(quad):
        h, slot = quad // 2, quad % 2
        if slot == 0:
            load_kv[h].wait()
            kt_v[...] = kv_v[h, :, :HD].T
            vt_v[...] = kv_v[h, :, HD:].T
            acc_k[...] = jnp.zeros_like(acc_k)
            acc_v[...] = jnp.zeros_like(acc_v)
        for copy in load_heads(quad):
            copy.wait()
        if quad + 1 < QUADS:
            for copy in load_heads(quad + 1):
                copy.start()
        if quad >= 2:
            store_heads(quad - 2).wait()
        cosine, sine, gain = cost_ref[...], sint_ref[...], wide_gain[...]
        key_row = lax.broadcasted_iota(jnp.int32, (TILE, TILE), 0)
        query_lane = lax.broadcasted_iota(jnp.int32, (TILE, TILE), 1)
        causal = key_row <= query_lane
        for head in range(HEADS):
            columns = slice(head * HD, (head + 1) * HD)
            raw = q_in[slot, :, columns].T.astype(F32)
            scale = lax.rsqrt(jnp.mean(raw * raw, axis=0, keepdims=True) + EPS)
            unit = raw * scale
            normed = unit * gain
            rot = normed * cosine + swap(normed) * sine
            query = (rot * (math.log2(math.e) / math.sqrt(HD))).astype(BF)
            weighted = (og_in[slot, :, columns].T.astype(F32) * coef_v[...]).astype(BF).astype(F32)
            scores = jnp.dot(kv_v[h, :, :HD], query, preferred_element_type=F32)
            weight = jnp.where(causal, jnp.exp2(scores), 0.0)
            low = weight.astype(BF)
            inverse = 1.0 / jnp.sum(weight, axis=0, keepdims=True)
            attended = jnp.dot(vt_v[...], low, preferred_element_type=F32) * inverse
            scaled = (weighted * inverse).astype(BF)
            dotted = jnp.sum(scaled.astype(F32) * attended, axis=0, keepdims=True)
            grad_probs = jnp.dot(kv_v[h, :, HD:], scaled, preferred_element_type=F32)
            grad_scores = (weight * (grad_probs - dotted)).astype(BF)
            acc_v[...] += lax.dot_general(low, scaled, contract_lanes, preferred_element_type=F32)
            acc_k[...] += lax.dot_general(
                grad_scores, query, contract_lanes, preferred_element_type=F32
            )
            grad_rot = jnp.dot(kt_v[...], grad_scores, preferred_element_type=F32) * (
                1.0 / math.sqrt(HD)
            )
            grad_normed = grad_rot * cosine - swap(grad_rot) * sine
            terms = grad_normed * unit
            acc_gain[...] += (
                terms[:, :128] + terms[:, 128:256] + terms[:, 256:384] + terms[:, 384:]
            )
            mean = jnp.mean(terms * gain, axis=0, keepdims=True)
            dq_v[slot, :, columns] = (scale * (grad_normed * gain - unit * mean)).astype(BF).T
        store_heads(quad).start()
        if slot == 1:
            gkv_v[h, :, :HD] = (acc_k[...] * math.log(2.0)).astype(BF)
            gkv_v[h, :, HD:] = acc_v[...].astype(BF)

    def spread(h):
        for k in range(1, NDP):
            to = (dp + k) % NDP
            sends.start(
                gkv_v.at[h, pl.ds(to * PIECE, PIECE), :], mids[h].at[dp],
                ex_send.at[h, 0, k], ex_recv.at[h, 0, k], (to, fs),
            )

        mids[h][dp] = gkv_v[h, pl.ds(pl.multiple_of(dp * PIECE, PIECE), PIECE), :]

    def forward(h):
        for k in range(1, NDP):
            ref = mids[h].at[(dp + NDP - k) % NDP]
            remote(ref, ref, ex_send.at[h, 0, k], ex_recv.at[h, 0, k], sibling).wait_recv()
        for k in range(NDP):
            to = (dp + k) % NDP
            if k == 0:
                back_v[h, dp] = mids[h][match(owner_ref, trainer_ref, to)]
            else:
                pass_v[h, k] = mids[h][match(owner_ref, trainer_ref, to)]
                sends.start(
                    pass_v.at[h, k], back_v.at[h, dp],
                    ex_send.at[h, 1, k], ex_recv.at[h, 1, k], (to, fs),
                )

    gain_parts = []

    def multiply(h):
        if h == 0:
            load_x.wait()
        for k in range(1, NDP):
            ref = back_v.at[h, (dp + NDP - k) % NDP]
            remote(ref, ref, ex_send.at[h, 1, k], ex_recv.at[h, 1, k], sibling).wait_recv()
        grads = back_v[h].reshape(TILE, 2 * HD)
        grad_rot = grads[:, :HD].astype(F32)
        raw = raw_ref[h]
        scale = lax.rsqrt(jnp.mean(raw * raw, axis=1, keepdims=True) + EPS)
        unit = raw * scale
        normed = grad_rot * cos_ref[...] - swap_lanes(grad_rot) * sin_ref[...]
        terms = normed * unit
        gain_parts.append(jnp.sum(terms, axis=0, keepdims=True))
        gained = normed * gain_ref[...]
        mean = jnp.mean(gained * unit, axis=1, keepdims=True)
        own = slice(2 * HD * h, 2 * HD * h + 2 * HD)
        key_grads = (scale * (gained - unit * mean)).astype(BF)
        g_v[:, own] = jnp.concatenate([key_grads, grads[:, HD:]], axis=1)

        @pl.loop(0, 4)
        def _(sy):
            start = pl.multiple_of(sy * 4 * SHARD, 4 * SHARD)
            part = jnp.dot(
                xt_v[pl.ds(start, 4 * SHARD), :], g_v[:, own], preferred_element_type=F32
            ).astype(BF)
            for sz in range(4):
                low, high = sz * SHARD, sz * SHARD + HALF
                for c in range(2):
                    dw_v[h, c, 0, sz, sy] = part[low:high, c * HD:(c + 1) * HD]
                    dw_v[h, c, 1, sy, sz] = part[high:low + SHARD, c * HD:(c + 1) * HD]

        for s in range(2):
            sends.start(
                dw_v.at[h, 1 - core, s], pair_v.at[h, s],
                rs_send.at[h, s, 0], rs_recv.at[h, s, 0], sibling,
            )

    def me(s, axis):
        return z if (s == 0) == (axis == 1) else y

    def ahead(s, axis, step):
        return at(0, step) if (s == 0) == (axis == 1) else at(step, 0)

    def send(h, s, slot, src, dst, axis, step):
        sends.start(src, dst, rs_send.at[h, s, slot], rs_recv.at[h, s, slot], ahead(s, axis, step))

    def landed(h, s, slot, ref):
        remote(ref, ref, rs_send.at[h, s, slot], rs_recv.at[h, s, slot], sibling).wait_recv()

    def add(ref, *others):
        total = ref[...].astype(F32)
        for other in others:
            total = total + other[...].astype(F32)
        ref[...] = total.astype(BF)

    def pair(h):
        for s in range(2):
            landed(h, s, 0, pair_v.at[h, s])
            mine = dw_v.at[h, core, s]
            for step in (2, 1, 3, 0):
                index = (me(s, 1) + step) % 4
                add(mine.at[index], pair_v.at[h, s, index])
                if step:
                    send(h, s, step, mine.at[index], r1_v.at[h, s, step - 1], 1, step)

    def cross(h):
        for s in range(2):
            for step in (1, 3, 2):
                landed(h, s, step, r1_v.at[h, s, step - 1])
            total = dw_v[h, core, s, me(s, 1)].astype(F32)
            for k in range(3):
                total = total + r1_v[h, s, k].astype(F32)
            q_v[h, s] = total.astype(BF)
            for step in (2, 1, 3):
                index = (me(s, 2) + step) % 4
                send(h, s, 3 + step, q_v.at[h, s, index], r2_v.at[h, s, step - 1], 2, step)

    def along_x(h):
        for s in range(2):
            for step in (1, 3, 2):
                landed(h, s, 3 + step, r2_v.at[h, s, step - 1])
            total = q_v[h, s, me(s, 2)].astype(F32)
            for k in range(3):
                total = total + r2_v[h, s, k].astype(F32)
            f_v[h, s * HALF:(s + 1) * HALF] = total.astype(BF)
        for k in range(1, 4):
            to = (cx + k) % 4
            sends.start(
                f_v.at[h, pl.ds(to * 80, 80), :], r7_v.at[h, k - 1],
                x_send.at[h, k - 1], x_recv.at[h, k - 1], (to * 2 + core, fs),
            )

    def spread_x(h):
        for k in range(1, 4):
            ref = r7_v.at[h, k - 1]
            remote(ref, ref, x_send.at[h, k - 1], x_recv.at[h, k - 1], sibling).wait_recv()
        rows = pl.ds(pl.multiple_of(cx * 80, 80), 80)
        total = f_v[h, rows, :].astype(F32)
        for k in range(3):
            total = total + r7_v[h, k].astype(F32)
        full_v[h, core, rows, :] = total.astype(BF)
        for k in range(1, NDP):
            ref = full_v.at[h, core, rows, :]
            sends.start(ref, ref, x_send.at[h, 2 + k], x_recv.at[h, 2 + k], ((dp + k) % NDP, fs))

    def finish(h):
        for k in range(1, NDP):
            source = (dp + NDP - k) % NDP
            ref = full_v.at[h, source % 2, pl.ds((source // 2) * 80, 80), :]
            remote(ref, ref, x_send.at[h, 2 + k], x_recv.at[h, 2 + k], sibling).wait_recv()
        outk_ref[:, h * HD:(h + 1) * HD] = full_v[h, 0].astype(F32)
        outv_ref[:, h * HD:(h + 1) * HD] = full_v[h, 1].astype(F32)

    groups = [
        (0, [((dp + k) % NDP, fs) for k in range(1, NDP)]),
        (7, [at(k, 0) for k in range(1, 4)]),
        (10, [at(0, k) for k in range(1, 4)]),
    ]

    def gains_out(stage):
        base, targets = groups[stage]
        for k, target in enumerate(targets):
            sends.start(
                gain_v.at[stage], gain_r.at[base + k], gn_send.at[base + k], gn_recv.at[base + k],
                target,
            )

    def gains_in(stage):
        base, targets = groups[stage]
        total = gain_v[stage]
        for k in range(len(targets)):
            ref = gain_r.at[base + k]
            remote(ref, ref, gn_send.at[base + k], gn_recv.at[base + k], sibling).wait_recv()
            total = total + gain_r[base + k]
        gain_v[stage + 1] = total

    def gains(stage):
        if stage == 0:
            row = lax.broadcasted_iota(jnp.int32, (8, HD), 0)
            keys = gain_parts[0] + gain_parts[1] + gain_parts[2] + gain_parts[3]
            queries = jnp.sum(acc_gain[...].T, axis=0, keepdims=True)
            gain_v[0] = jnp.where(row == 0, queries, jnp.where(row == 1, keys, 0.0))
        else:
            gains_in(stage - 1)
        if stage < 3:
            gains_out(stage)
        else:
            gq_out[...] = gain_v[3, 0:1]
            gk_out[...] = gain_v[3, 1:2]

    def then_gains(stage_function, stage):
        def both(h):
            stage_function(h)
            if h == KVH - 1:
                gains(stage)

        return both

    stages = [
        spread, forward, then_gains(multiply, 0), then_gains(pair, 1), then_gains(cross, 2),
        then_gains(along_x, 3), spread_x, finish,
    ]
    stores = []

    def hidden(part):
        if part == 0:
            load_w.wait()
        if part >= 2:
            stores[part - 2].wait()
        wide = D // 4
        columns = slice(part * wide, (part + 1) * wide)
        hidden_v[part % 2] = jnp.dot(
            g_v[...], wt_v[:, :, columns].reshape(2 * KVH * HD, wide), preferred_element_type=F32
        ).astype(BF)
        copy = pltpu.make_async_copy(
            hidden_v.at[part % 2], hidden_hbm.at[:, pl.ds(part * wide, wide)],
            load_sem.at[KVH + 2 + part],
        )
        copy.start()
        stores.append(copy)

    last = 2 * KVH - 1
    hidden_from = last + 2
    for slot in range(last + len(stages)):
        if slot < QUADS:
            attend(slot)
        for h in reversed(range(KVH)):
            step = slot - (2 * h + 1)
            if 0 <= step < len(stages):
                stages[step](h)
        if 0 <= slot - hidden_from < 4:
            hidden(slot - hidden_from)
    sends.drain()
    for quad in (QUADS - 2, QUADS - 1):
        store_heads(quad).wait()
    for copy in stores[2:]:
        copy.wait()


def reduce_call(*operands):
    any_spec = pl.BlockSpec(memory_space=pl.ANY)
    vmem_spec = pl.BlockSpec(memory_space=pltpu.VMEM)
    return pl.pallas_call(
        reduce_kernel,
        out_shape=(
            jax.ShapeDtypeStruct((TILE, D), BF),
            jax.ShapeDtypeStruct((TILE, QH * HD), BF),
            jax.ShapeDtypeStruct((SHARD, KVH * HD), F32),
            jax.ShapeDtypeStruct((SHARD, KVH * HD), F32),
            jax.ShapeDtypeStruct((1, HD), F32),
            jax.ShapeDtypeStruct((1, HD), F32),
        ),
        in_specs=[pl.BlockSpec(memory_space=pltpu.SMEM)] * 4 + [any_spec] * 5 + [vmem_spec] * 7,
        out_specs=(any_spec,) * 2 + (vmem_spec,) * 4,
        scratch_shapes=[
            pltpu.VMEM((2, TILE, HEADS * HD), BF),
            pltpu.VMEM((2, TILE, HEADS * HD), BF),
            pltpu.VMEM((2, TILE, HEADS * HD), BF),
            pltpu.VMEM((KVH, TILE, 2 * HD), BF),
            pltpu.VMEM((KVH, TILE, 2 * HD), BF),
            pltpu.VMEM((HD, TILE), BF),
            pltpu.VMEM((HD, TILE), BF),
            pltpu.VMEM((TILE, HD), F32),
            pltpu.VMEM((TILE, HD), F32),
            pltpu.VMEM((HD, HD), F32),
            pltpu.VMEM((HD, TILE), F32),
            pltpu.VMEM((1, TILE), F32),
            pltpu.VMEM((D, TILE), BF),
            pltpu.VMEM((2 * KVH, HD, D), BF),
            pltpu.VMEM((TILE, 2 * KVH * HD), BF),
            pltpu.VMEM((2, TILE, D // 4), BF),
            *[pltpu.VMEM((NDP, PIECE, 2 * HD), BF)] * KVH,
            pltpu.VMEM((KVH, NDP, PIECE, 2 * HD), BF),
            pltpu.VMEM((KVH, NDP, PIECE, 2 * HD), BF),
            pltpu.VMEM((KVH, 2, 2, 4, 4, HALF, HD), BF),
            pltpu.VMEM((KVH, 2, 4, 4, HALF, HD), BF),
            pltpu.VMEM((KVH, 2, 3, 4, HALF, HD), BF),
            pltpu.VMEM((KVH, 2, 3, HALF, HD), BF),
            pltpu.VMEM((KVH, 2, 4, HALF, HD), BF),
            pltpu.VMEM((KVH, SHARD, HD), BF),
            pltpu.VMEM((KVH, 3, 80, HD), BF),
            pltpu.VMEM((KVH, 2, SHARD, HD), BF),
            pltpu.VMEM((4, 8, HD), F32),
            pltpu.VMEM((13, 8, HD), F32),
            pltpu.SemaphoreType.DMA((KVH + 6,)),
            pltpu.SemaphoreType.DMA((3, 2)),
            pltpu.SemaphoreType.DMA((KVH, 2, NDP)),
            pltpu.SemaphoreType.DMA((KVH, 2, NDP)),
            pltpu.SemaphoreType.DMA((KVH, 2, 7)),
            pltpu.SemaphoreType.DMA((KVH, 2, 7)),
            pltpu.SemaphoreType.DMA((KVH, 10)),
            pltpu.SemaphoreType.DMA((KVH, 10)),
            pltpu.SemaphoreType.DMA((13,)),
            pltpu.SemaphoreType.DMA((13,)),
        ],
        compiler_params=pltpu.CompilerParams(
            collective_id=1, has_side_effects=True, vmem_limit_bytes=VMEM_LIMIT
        ),
        name="attention_return_reduce",
    )(*operands)


def per_device(
    rollout_hidden, key_weight, value_weight, key_gain, query_gain, queries, out_grad, rewards,
    response_lengths, rollout_owner, train_shard, pack_offsets,
):
    del pack_offsets
    cosine, sine = rope_arrays()
    key_gain_row = key_gain.reshape(1, HD)
    wt, kv, raw, xt = gather_call(
        rollout_hidden, key_weight, value_weight, key_gain_row, cosine, sine,
        rollout_owner, train_shard,
    )
    d_hidden, d_queries, grad_key_weight, grad_value_weight, query_gain_grad, key_gain_grad = (
        reduce_call(
            rewards, response_lengths, rollout_owner, train_shard,
            queries, out_grad, kv, xt, wt, raw, query_gain.reshape(1, HD), key_gain_row,
            cosine, sine, np.ascontiguousarray(cosine.T), np.ascontiguousarray(sine.T),
        )
    )
    return (
        d_hidden, d_queries, grad_key_weight, grad_value_weight,
        query_gain_grad.reshape(HD), key_gain_grad.reshape(HD),
    )


def solution(mesh):
    rows, split = P(("dp", "fsdp"), None), P("fsdp", None)
    return jax.shard_map(
        per_device,
        mesh=mesh,
        in_specs=(rows, split, split, P(), P(), rows, rows, split, split, split, split, split),
        out_specs=(rows, rows, split, split, P(), P()),
        check_vma=False,
    )
```

```python
import functools
import math

import jax
import jax.numpy as jnp
import numpy as np
from jax import lax
from jax.experimental import pallas as pl
from jax.experimental.pallas import tpu as pltpu
from jax.sharding import PartitionSpec as P

MESH = pl.DeviceIdType.MESH
BF, F32 = jnp.bfloat16, jnp.float32
HD = 128
GSIZE = 4
TILE = 512
D = 5120
KVH = 4
QH = 32
GROUP = QH // KVH
NDP = 8
SHARD = 320
HALF = SHARD // 2
PIECE = TILE // NDP
EPS = 1e-06
VMEM_LIMIT = 62 * 1024 * 1024


def rope_arrays():
    half = HD // 2
    frequency = 1000000.0 ** (-np.arange(half, dtype=np.float64) / half)
    angles = np.arange(TILE, dtype=np.float64)[:, None] * frequency[None, :]
    cosine, sine = np.cos(angles), np.sin(angles)
    return (
        np.concatenate([cosine, cosine], axis=1).astype(np.float32),
        np.concatenate([-sine, sine], axis=1).astype(np.float32),
    )


def place():
    dp, fs = lax.axis_index("dp"), lax.axis_index("fsdp")
    return dp, fs, dp // 2, dp % 2, fs // 4, fs % 4


def remote(src, dst, send, recv, device):
    return pltpu.make_async_remote_copy(
        src_ref=src, dst_ref=dst, send_sem=send, recv_sem=recv, device_id=device, device_id_type=MESH
    )


def entry_barrier(peers):
    barrier = pltpu.get_barrier_semaphore()
    for peer in peers:
        pl.semaphore_signal(barrier, inc=1, device_id=peer, device_id_type=MESH)
    pl.semaphore_wait(barrier, len(peers))


def match(labels_ref, values_ref, label):
    found = jnp.int32(0)
    for r in range(NDP):
        found = jnp.where(labels_ref[0, r] == label, values_ref[0, r], found)
    return found


def swap_lanes(values):
    return pltpu.roll(values, HD // 2, axis=1)


class Sends:
    def __init__(self):
        self.pending = []

    def start(self, *args, group=None):
        copy = remote(*args)
        copy.start()
        self.pending.append((group, copy))

    def drain(self, group=None):
        rest = []
        for name, copy in self.pending:
            if group is None or name == group:
                copy.wait_send()
            else:
                rest.append((name, copy))
        self.pending = rest


HEADS = 4
QUADS = QH // HEADS


def layer_kernel(
    rewards_ref, length_ref, owner_ref, trainer_ref,
    x_hbm, kw_hbm, vw_hbm, q_hbm, og_hbm,
    qgain_ref, kgain_ref, cos_ref, sin_ref, cost_ref, sint_ref,
    hidden_hbm, dq_hbm, outk_ref, outv_ref, gq_out, gk_out,
    x_v, w_v, xt_v, tile_v, om0, om1, om2, om3, out_v, raw_v,
    q_in, og_in, dq_v, kv_v, kt_v, vt_v, acc_k, acc_v, acc_gain, wide_gain, coef_v,
    mid0, mid1, mid2, mid3, back_v, g_v, dw_v, give_v, pair_v, r1_v, r2_v, q_v, f_v, r7_v, full_v,
    gain_v, gain_r,
    load_sem, head_sem, ag_send, ag_recv, gx_send, gx_recv, ex_send, ex_recv, rs_send, rs_recv,
    x_send, x_recv, gn_send, gn_recv,
):
    out_mids = (om0, om1, om2, om3)
    mids = (mid0, mid1, mid2, mid3)
    dp, fs, cx, core, y, z = place()
    sibling = (dp + 1 - 2 * core, fs)

    def at(dy, dz):
        return (dp, ((y + dy) % 4) * 4 + (z + dz) % 4)

    peers = [((dp + k) % NDP, fs) for k in range(1, NDP)]
    peers += [at(k, 0) for k in range(1, 4)] + [at(0, k) for k in range(1, 4)]
    load_x = pltpu.make_async_copy(x_hbm, x_v, load_sem.at[KVH])

    def load_w(h, source):
        return pltpu.make_async_copy(
            source.at[:, pl.ds(h * HD, HD)], w_v.at[core, h, y, z], load_sem.at[h]
        )

    for h in range(KVH):
        @pl.when(core == 0)
        def _():
            load_w(h, kw_hbm).start()

        @pl.when(core == 1)
        def _():
            load_w(h, vw_hbm).start()

    load_x.start()
    entry_barrier(peers)
    for h in range(KVH):
        load_w(h, kw_hbm).wait()
    sends = Sends()

    def block(h, s, d1, d2, low, rows):
        dy, dz = (d1, d2) if s == 0 else (d2, d1)
        return w_v.at[core, h, (y + dy) % 4, (z + dz) % 4, pl.ds(s * HALF + low, rows), :]

    def ag_ahead(s, axis, step):
        return at(step, 0) if (s == 0) == (axis == 1) else at(0, step)

    def pass_on(h, s, axis, step, ref, slot):
        sends.start(ref, ref, ag_send.at[h, s, slot], ag_recv.at[h, s, slot], ag_ahead(s, axis, step))

    def got(h, s, ref, slot):
        remote(ref, ref, ag_send.at[h, s, slot], ag_recv.at[h, s, slot], sibling).wait_recv()

    quarter = HALF // 2

    def both_ways(h, s, b):
        ref = block(h, s, b, 0, 0, HALF)
        pass_on(h, s, 2, 1, ref, 4 + 4 * b)
        pass_on(h, s, 2, 3, ref, 5 + 4 * b)

    def own(h):
        for s in range(2):
            ref = block(h, s, 0, 0, 0, HALF)
            pass_on(h, s, 1, 1, ref, 0)
            pass_on(h, s, 1, 3, ref, 1)
        for s in range(2):
            both_ways(h, s, 0)

    def near_blocks(h):
        for s in range(2):
            got(h, s, block(h, s, 3, 0, 0, HALF), 0)
            pass_on(h, s, 1, 1, block(h, s, 3, 0, 0, quarter), 2)
            got(h, s, block(h, s, 1, 0, 0, HALF), 1)
            pass_on(h, s, 1, 3, block(h, s, 1, 0, quarter, quarter), 3)
        for s in range(2):
            both_ways_from(h, s)

    def both_ways_from(h, s):
        for b in (3, 1):
            both_ways(h, s, b)

    def far_block(h):
        for s in range(2):
            got(h, s, block(h, s, 2, 0, 0, quarter), 2)
            got(h, s, block(h, s, 2, 0, quarter, quarter), 3)
            both_ways(h, s, 2)

    def relay(h, blocks):
        for b in blocks:
            for s in range(2):
                got(h, s, block(h, s, b, 3, 0, HALF), 4 + 4 * b)
                pass_on(h, s, 2, 1, block(h, s, b, 3, 0, quarter), 6 + 4 * b)
                got(h, s, block(h, s, b, 1, 0, HALF), 5 + 4 * b)
                pass_on(h, s, 2, 3, block(h, s, b, 1, quarter, quarter), 7 + 4 * b)

    def share(h):
        for b in (0, 3, 1, 2):
            for s in range(2):
                got(h, s, block(h, s, b, 2, 0, quarter), 6 + 4 * b)
                got(h, s, block(h, s, b, 2, quarter, quarter), 7 + 4 * b)
        sends.start(
            w_v.at[core, h], w_v.at[core, h], gx_send.at[h, 0, 0], gx_recv.at[h, 0, 0], sibling
        )

    def project(h):
        other = w_v.at[1 - core, h]
        remote(other, other, gx_send.at[h, 0, 0], gx_recv.at[h, 0, 0], sibling).wait_recv()
        @pl.loop(0, 2)
        def _(part):
            rows = pl.ds(pl.multiple_of(part * 256, 256), 256)
            weights = jnp.concatenate(
                [w_v[0, h].reshape(D, HD), w_v[1, h].reshape(D, HD)], axis=1
            )
            both = jnp.dot(x_v[rows, :], weights, preferred_element_type=F32)
            raw = both[:, :HD]
            raw_v[h, rows, :] = raw
            scale = lax.rsqrt(jnp.mean(raw * raw, axis=1, keepdims=True) + EPS)
            normed = raw * scale * kgain_ref[...]
            rot = normed * cos_ref[rows, :] + swap_lanes(normed) * sin_ref[rows, :]
            tile_v[h, rows, :] = jnp.concatenate([rot, both[:, HD:]], axis=1).astype(BF)

        for k in range(1, NDP):
            to = (dp + k) % NDP
            sends.start(
                tile_v.at[h, pl.ds(to * PIECE, PIECE), :], out_mids[h].at[dp],
                gx_send.at[h, 0, k], gx_recv.at[h, 0, k], (to, fs), group=("tile", h),
            )
        out_mids[h][dp] = tile_v[h, pl.ds(pl.multiple_of(dp * PIECE, PIECE), PIECE), :]

    def give(h):
        for k in range(1, NDP):
            ref = out_mids[h].at[(dp + NDP - k) % NDP]
            remote(ref, ref, gx_send.at[h, 0, k], gx_recv.at[h, 0, k], sibling).wait_recv()
        for k in range(NDP):
            to = (dp + k) % NDP
            out_v[h, k] = out_mids[h][match(trainer_ref, owner_ref, to)]
            ref = kv_v.at[h, pl.ds(dp * PIECE, PIECE), :]
            if k == 0:
                kv_v[h, pl.ds(pl.multiple_of(dp * PIECE, PIECE), PIECE), :] = out_v[h, k]
            else:
                sends.start(
                    out_v.at[h, k], ref, gx_send.at[h, 1, k], gx_recv.at[h, 1, k], (to, fs),
                    group=("out", h),
                )

    def arrive(h):
        for k in range(1, NDP):
            ref = kv_v.at[h, pl.ds(((dp + NDP - k) % NDP) * PIECE, PIECE), :]
            remote(ref, ref, gx_send.at[h, 1, k], gx_recv.at[h, 1, k], sibling).wait_recv()

    def turn(h):
        if h == 0:
            load_x.wait()

        step = D // KVH
        xt_v[h * step:(h + 1) * step, :] = x_v[:, h * step:(h + 1) * step].T

    def relay_early(h):
        relay(h, (0, 3, 1))

    def relay_late(h):
        relay(h, (2,))

    width = HEADS * HD

    def load_heads(quad):
        columns, slot = pl.ds(quad * width, width), quad % 2
        return (
            pltpu.make_async_copy(q_hbm.at[:, columns], q_in.at[slot], head_sem.at[0, slot]),
            pltpu.make_async_copy(og_hbm.at[:, columns], og_in.at[slot], head_sem.at[1, slot]),
        )

    def store_heads(quad):
        columns, slot = pl.ds(quad * width, width), quad % 2
        return pltpu.make_async_copy(dq_v.at[slot], dq_hbm.at[:, columns], head_sem.at[2, slot])

    for copy in load_heads(0):
        copy.start()

    acc_gain[...] = jnp.zeros_like(acc_gain)
    column = jnp.broadcast_to(qgain_ref[...], (HD, HD)).T
    wide_gain[...] = jnp.concatenate([column] * (TILE // HD), axis=1)
    length, factor = jnp.int32(0), jnp.float32(0.0)
    for r in range(NDP):
        group = (r // GSIZE) * GSIZE
        total = rewards_ref[0, group]
        for member in range(1, GSIZE):
            total = total + rewards_ref[0, group + member]
        mine = trainer_ref[0, r] == dp
        length = jnp.where(mine, length_ref[0, r], length)
        factor = jnp.where(mine, rewards_ref[0, r] - total * (1.0 / GSIZE), factor)
    position = lax.broadcasted_iota(jnp.int32, (1, TILE), 1)
    coef_v[...] = jnp.where(position < length, factor, 0.0)
    half = HD // 2

    def swap(values):
        return jnp.concatenate([values[half:], values[:half]], axis=0)

    contract_lanes = (((1,), (1,)), ((), ()))

    def attend(quad):
        h, slot = quad // 2, quad % 2
        if slot == 0:
            kt_v[...] = kv_v[h, :, :HD].T
            vt_v[...] = kv_v[h, :, HD:].T
            acc_k[...] = jnp.zeros_like(acc_k)
            acc_v[...] = jnp.zeros_like(acc_v)
        for copy in load_heads(quad):
            copy.wait()
        if quad + 1 < QUADS:
            for copy in load_heads(quad + 1):
                copy.start()
        if quad >= 2:
            store_heads(quad - 2).wait()
        cosine, sine, gain = cost_ref[...], sint_ref[...], wide_gain[...]
        key_row = lax.broadcasted_iota(jnp.int32, (TILE, TILE), 0)
        query_lane = lax.broadcasted_iota(jnp.int32, (TILE, TILE), 1)
        causal = key_row <= query_lane
        for head in range(HEADS):
            columns = slice(head * HD, (head + 1) * HD)
            raw = q_in[slot, :, columns].T.astype(F32)
            scale = lax.rsqrt(jnp.mean(raw * raw, axis=0, keepdims=True) + EPS)
            unit = raw * scale
            normed = unit * gain
            rot = normed * cosine + swap(normed) * sine
            query = (rot * (math.log2(math.e) / math.sqrt(HD))).astype(BF)
            weighted = (og_in[slot, :, columns].T.astype(F32) * coef_v[...]).astype(BF).astype(F32)
            scores = jnp.dot(kv_v[h, :, :HD], query, preferred_element_type=F32)
            weight = jnp.where(causal, jnp.exp2(scores), 0.0)
            low = weight.astype(BF)
            inverse = 1.0 / jnp.sum(weight, axis=0, keepdims=True)
            attended = jnp.dot(vt_v[...], low, preferred_element_type=F32) * inverse
            scaled = (weighted * inverse).astype(BF)
            dotted = jnp.sum(scaled.astype(F32) * attended, axis=0, keepdims=True)
            grad_probs = jnp.dot(kv_v[h, :, HD:], scaled, preferred_element_type=F32)
            grad_scores = (weight * (grad_probs - dotted)).astype(BF)
            acc_v[...] += lax.dot_general(low, scaled, contract_lanes, preferred_element_type=F32)
            acc_k[...] += lax.dot_general(
                grad_scores, query, contract_lanes, preferred_element_type=F32
            )
            grad_rot = jnp.dot(kt_v[...], grad_scores, preferred_element_type=F32) * (
                1.0 / math.sqrt(HD)
            )
            grad_normed = grad_rot * cosine - swap(grad_rot) * sine
            terms = grad_normed * unit
            acc_gain[...] += (
                terms[:, :128] + terms[:, 128:256] + terms[:, 256:384] + terms[:, 384:]
            )
            mean = jnp.mean(terms * gain, axis=0, keepdims=True)
            dq_v[slot, :, columns] = (scale * (grad_normed * gain - unit * mean)).astype(BF).T
        store_heads(quad).start()
        if slot == 1:
            sends.drain(("tile", h))
            tile_v[h, :, :HD] = (acc_k[...] * math.log(2.0)).astype(BF)
            tile_v[h, :, HD:] = acc_v[...].astype(BF)

    def spread(h):
        for k in range(1, NDP):
            to = (dp + k) % NDP
            sends.start(
                tile_v.at[h, pl.ds(to * PIECE, PIECE), :], mids[h].at[dp],
                ex_send.at[h, 0, k], ex_recv.at[h, 0, k], (to, fs),
            )

        mids[h][dp] = tile_v[h, pl.ds(pl.multiple_of(dp * PIECE, PIECE), PIECE), :]

    def forward(h):
        sends.drain(("out", h))
        for k in range(1, NDP):
            ref = mids[h].at[(dp + NDP - k) % NDP]
            remote(ref, ref, ex_send.at[h, 0, k], ex_recv.at[h, 0, k], sibling).wait_recv()
        for k in range(NDP):
            to = (dp + k) % NDP
            if k == 0:
                back_v[h, dp] = mids[h][match(owner_ref, trainer_ref, to)]
            else:
                out_v[h, k] = mids[h][match(owner_ref, trainer_ref, to)]
                sends.start(
                    out_v.at[h, k], back_v.at[h, dp],
                    ex_send.at[h, 1, k], ex_recv.at[h, 1, k], (to, fs),
                )

    gain_parts = []

    def multiply(h):
        for k in range(1, NDP):
            ref = back_v.at[h, (dp + NDP - k) % NDP]
            remote(ref, ref, ex_send.at[h, 1, k], ex_recv.at[h, 1, k], sibling).wait_recv()
        grads = back_v[h].reshape(TILE, 2 * HD)
        grad_rot = grads[:, :HD].astype(F32)
        raw = raw_v[h]
        scale = lax.rsqrt(jnp.mean(raw * raw, axis=1, keepdims=True) + EPS)
        unit = raw * scale
        normed = grad_rot * cos_ref[...] - swap_lanes(grad_rot) * sin_ref[...]
        terms = normed * unit
        gain_parts.append(jnp.sum(terms, axis=0, keepdims=True))
        gained = normed * kgain_ref[...]
        mean = jnp.mean(gained * unit, axis=1, keepdims=True)
        own = slice(2 * HD * h, 2 * HD * h + 2 * HD)
        key_grads = (scale * (gained - unit * mean)).astype(BF)
        g_v[:, own] = jnp.concatenate([key_grads, grads[:, HD:]], axis=1)

        if h >= 2:
            sends.drain(("give", h - 2))

        @pl.loop(0, 4)
        def _(sy):
            start = pl.multiple_of(sy * 4 * SHARD, 4 * SHARD)
            part = jnp.dot(
                xt_v[pl.ds(start, 4 * SHARD), :], g_v[:, own], preferred_element_type=F32
            ).astype(BF)
            first, second = part[:, :HD], part[:, HD:]
            mine = jnp.where(core == 0, first, second)
            other = jnp.where(core == 0, second, first)
            for sz in range(4):
                low, high = sz * SHARD, sz * SHARD + HALF
                dw_v[h, 0, sz, sy] = mine[low:high]
                dw_v[h, 1, sy, sz] = mine[high:low + SHARD]
                give_v[h % 2, 0, sz, sy] = other[low:high]
                give_v[h % 2, 1, sy, sz] = other[high:low + SHARD]

        for s in range(2):
            sends.start(
                give_v.at[h % 2, s], pair_v.at[h, s],
                rs_send.at[h, s, 0], rs_recv.at[h, s, 0], sibling, group=("give", h),
            )

    def me(s, axis):
        return z if (s == 0) == (axis == 1) else y

    def ahead(s, axis, step):
        return at(0, step) if (s == 0) == (axis == 1) else at(step, 0)

    def send(h, s, slot, src, dst, axis, step):
        sends.start(src, dst, rs_send.at[h, s, slot], rs_recv.at[h, s, slot], ahead(s, axis, step))

    def landed(h, s, slot, ref):
        remote(ref, ref, rs_send.at[h, s, slot], rs_recv.at[h, s, slot], sibling).wait_recv()

    def add(ref, *others):
        total = ref[...].astype(F32)
        for other in others:
            total = total + other[...].astype(F32)
        ref[...] = total.astype(BF)

    def pair(h):
        for s in range(2):
            landed(h, s, 0, pair_v.at[h, s])
            mine = dw_v.at[h, s]
            for step in (2, 1, 3, 0):
                index = (me(s, 1) + step) % 4
                add(mine.at[index], pair_v.at[h, s, index])
                if step:
                    send(h, s, step, mine.at[index], r1_v.at[h, s, step - 1], 1, step)

    def cross(h):
        for s in range(2):
            for step in (1, 3, 2):
                landed(h, s, step, r1_v.at[h, s, step - 1])
            total = dw_v[h, s, me(s, 1)].astype(F32)
            for k in range(3):
                total = total + r1_v[h, s, k].astype(F32)
            q_v[h, s] = total.astype(BF)
            for step in (2, 1, 3):
                index = (me(s, 2) + step) % 4
                send(h, s, 3 + step, q_v.at[h, s, index], r2_v.at[h, s, step - 1], 2, step)

    def along_x(h):
        for s in range(2):
            for step in (1, 3, 2):
                landed(h, s, 3 + step, r2_v.at[h, s, step - 1])
            total = q_v[h, s, me(s, 2)].astype(F32)
            for k in range(3):
                total = total + r2_v[h, s, k].astype(F32)
            f_v[h, s * HALF:(s + 1) * HALF] = total.astype(BF)
        for k in range(1, 4):
            to = (cx + k) % 4
            sends.start(
                f_v.at[h, pl.ds(to * 80, 80), :], r7_v.at[h, k - 1],
                x_send.at[h, k - 1], x_recv.at[h, k - 1], (to * 2 + core, fs),
            )

    def spread_x(h):
        for k in range(1, 4):
            ref = r7_v.at[h, k - 1]
            remote(ref, ref, x_send.at[h, k - 1], x_recv.at[h, k - 1], sibling).wait_recv()
        rows = pl.ds(pl.multiple_of(cx * 80, 80), 80)
        total = f_v[h, rows, :].astype(F32)
        for k in range(3):
            total = total + r7_v[h, k].astype(F32)
        full_v[h, core, rows, :] = total.astype(BF)
        for k in range(1, NDP):
            ref = full_v.at[h, core, rows, :]
            sends.start(ref, ref, x_send.at[h, 2 + k], x_recv.at[h, 2 + k], ((dp + k) % NDP, fs))

    def finish(h):
        for k in range(1, NDP):
            source = (dp + NDP - k) % NDP
            ref = full_v.at[h, source % 2, pl.ds((source // 2) * 80, 80), :]
            remote(ref, ref, x_send.at[h, 2 + k], x_recv.at[h, 2 + k], sibling).wait_recv()
        outk_ref[:, h * HD:(h + 1) * HD] = full_v[h, 0].astype(F32)
        outv_ref[:, h * HD:(h + 1) * HD] = full_v[h, 1].astype(F32)

    groups = [
        (0, [((dp + k) % NDP, fs) for k in range(1, NDP)]),
        (7, [at(k, 0) for k in range(1, 4)]),
        (10, [at(0, k) for k in range(1, 4)]),
    ]

    def gains_out(stage):
        base, targets = groups[stage]
        for k, target in enumerate(targets):
            sends.start(
                gain_v.at[stage], gain_r.at[base + k], gn_send.at[base + k], gn_recv.at[base + k],
                target,
            )

    def gains_in(stage):
        base, targets = groups[stage]
        total = gain_v[stage]
        for k in range(len(targets)):
            ref = gain_r.at[base + k]
            remote(ref, ref, gn_send.at[base + k], gn_recv.at[base + k], sibling).wait_recv()
            total = total + gain_r[base + k]
        gain_v[stage + 1] = total

    def gains(stage):
        if stage == 0:
            row = lax.broadcasted_iota(jnp.int32, (8, HD), 0)
            keys = gain_parts[0] + gain_parts[1] + gain_parts[2] + gain_parts[3]
            queries = jnp.sum(acc_gain[...].T, axis=0, keepdims=True)
            gain_v[0] = jnp.where(row == 0, queries, jnp.where(row == 1, keys, 0.0))
        else:
            gains_in(stage - 1)
        if stage < 3:
            gains_out(stage)
        else:
            gq_out[...] = gain_v[3, 0:1]
            gk_out[...] = gain_v[3, 1:2]

    def then_gains(stage_function, stage):
        def both(h):
            stage_function(h)
            if h == KVH - 1:
                gains(stage)

        return both

    stages = [
        spread, forward, then_gains(multiply, 0), then_gains(pair, 1), then_gains(cross, 2),
        then_gains(along_x, 3), spread_x, finish,
    ]
    stores = []

    def hidden(part):
        wide = D // 4
        columns = slice(part * wide, (part + 1) * wide)
        weights = jnp.concatenate(
            [w_v[c, h, part].reshape(wide, HD) for h in range(KVH) for c in range(2)], axis=1
        )
        x_v[:, columns] = lax.dot_general(
            g_v[...], weights, contract_lanes, preferred_element_type=F32
        ).astype(BF)
        copy = pltpu.make_async_copy(
            x_v.at[:, pl.ds(part * wide, wide)], hidden_hbm.at[:, pl.ds(part * wide, wide)],
            load_sem.at[KVH + 1 + part],
        )
        copy.start()
        stores.append(copy)

    out_stages = [
        own, near_blocks, far_block, relay_early, relay_late, share, project, give, arrive
    ]
    begin = len(out_stages)
    last = begin + 2 * KVH - 1
    for tick in range(last + len(stages)):
        if 0 <= tick - begin < QUADS:
            attend(tick - begin)
        for h in reversed(range(KVH)):
            step = tick - 2 * h
            if 0 <= step < len(out_stages):
                out_stages[step](h)
            step = tick - (begin + 2 * h + 1)
            if 0 <= step < len(stages):
                stages[step](h)
        if 1 <= tick <= KVH:
            turn(tick - 1)
        if 0 <= tick - (last + 2) < 4:
            hidden(tick - (last + 2))
    sends.drain()
    for quad in (QUADS - 2, QUADS - 1):
        store_heads(quad).wait()
    for copy in stores:
        copy.wait()


def layer_call(*operands):
    any_spec = pl.BlockSpec(memory_space=pl.ANY)
    vmem_spec = pl.BlockSpec(memory_space=pltpu.VMEM)
    heads = pltpu.VMEM((2, TILE, HEADS * HD), BF)
    tiles = pltpu.VMEM((KVH, TILE, 2 * HD), BF)
    pieces = pltpu.VMEM((NDP, PIECE, 2 * HD), BF)
    all_pieces = pltpu.VMEM((KVH, NDP, PIECE, 2 * HD), BF)
    dma = pltpu.SemaphoreType.DMA
    return pl.pallas_call(
        layer_kernel,
        out_shape=(
            jax.ShapeDtypeStruct((TILE, D), BF),
            jax.ShapeDtypeStruct((TILE, QH * HD), BF),
            jax.ShapeDtypeStruct((SHARD, KVH * HD), F32),
            jax.ShapeDtypeStruct((SHARD, KVH * HD), F32),
            jax.ShapeDtypeStruct((1, HD), F32),
            jax.ShapeDtypeStruct((1, HD), F32),
        ),
        in_specs=[pl.BlockSpec(memory_space=pltpu.SMEM)] * 4 + [any_spec] * 5 + [vmem_spec] * 6,
        out_specs=(any_spec,) * 2 + (vmem_spec,) * 4,
        scratch_shapes=[
            pltpu.VMEM((TILE, D), BF),
            pltpu.VMEM((2, KVH, 4, 4, SHARD, HD), BF),
            pltpu.VMEM((D, TILE), BF),
            tiles, pieces, pieces, pieces, pieces, all_pieces,
            pltpu.VMEM((KVH, TILE, HD), F32),
            heads, heads, heads, tiles,
            pltpu.VMEM((HD, TILE), BF),
            pltpu.VMEM((HD, TILE), BF),
            pltpu.VMEM((TILE, HD), F32),
            pltpu.VMEM((TILE, HD), F32),
            pltpu.VMEM((HD, HD), F32),
            pltpu.VMEM((HD, TILE), F32),
            pltpu.VMEM((1, TILE), F32),
            pieces, pieces, pieces, pieces, all_pieces,
            pltpu.VMEM((TILE, 2 * KVH * HD), BF),
            pltpu.VMEM((KVH, 2, 4, 4, HALF, HD), BF),
            pltpu.VMEM((2, 2, 4, 4, HALF, HD), BF),
            pltpu.VMEM((KVH, 2, 4, 4, HALF, HD), BF),
            pltpu.VMEM((KVH, 2, 3, 4, HALF, HD), BF),
            pltpu.VMEM((KVH, 2, 3, HALF, HD), BF),
            pltpu.VMEM((KVH, 2, 4, HALF, HD), BF),
            pltpu.VMEM((KVH, SHARD, HD), BF),
            pltpu.VMEM((KVH, 3, 80, HD), BF),
            pltpu.VMEM((KVH, 2, SHARD, HD), BF),
            pltpu.VMEM((4, 8, HD), F32),
            pltpu.VMEM((13, 8, HD), F32),
            dma((KVH + 5,)), dma((3, 2)),
            dma((KVH, 2, 20)), dma((KVH, 2, 20)),
            dma((KVH, 2, NDP)), dma((KVH, 2, NDP)),
            dma((KVH, 2, NDP)), dma((KVH, 2, NDP)),
            dma((KVH, 2, 7)), dma((KVH, 2, 7)),
            dma((KVH, 10)), dma((KVH, 10)),
            dma((13,)), dma((13,)),
        ],
        compiler_params=pltpu.CompilerParams(
            collective_id=0, has_side_effects=True, vmem_limit_bytes=VMEM_LIMIT
        ),
        name="layer_backward",
    )(*operands)


def per_device(
    rollout_hidden, key_weight, value_weight, key_gain, query_gain, queries, out_grad, rewards,
    response_lengths, rollout_owner, train_shard, pack_offsets,
):
    del pack_offsets
    cosine, sine = rope_arrays()
    d_hidden, d_queries, grad_key_weight, grad_value_weight, query_gain_grad, key_gain_grad = (
        layer_call(
            rewards, response_lengths, rollout_owner, train_shard,
            rollout_hidden, key_weight, value_weight, queries, out_grad,
            query_gain.reshape(1, HD), key_gain.reshape(1, HD),
            cosine, sine, np.ascontiguousarray(cosine.T), np.ascontiguousarray(sine.T),
        )
    )
    return (
        d_hidden, d_queries, grad_key_weight, grad_value_weight,
        query_gain_grad.reshape(HD), key_gain_grad.reshape(HD),
    )


def solution(mesh):
    rows, split = P(("dp", "fsdp"), None), P("fsdp", None)
    return jax.shard_map(
        per_device,
        mesh=mesh,
        in_specs=(rows, split, split, P(), P(), rows, rows, split, split, split, split, split),
        out_specs=(rows, rows, split, split, P(), P()),
        check_vma=False,
    )
```

```python
import functools
import math

import jax
import jax.numpy as jnp
import numpy as np
from jax import lax
from jax.experimental import pallas as pl
from jax.experimental.pallas import tpu as pltpu
from jax.sharding import PartitionSpec as P

MESH = pl.DeviceIdType.MESH
BF, F32 = jnp.bfloat16, jnp.float32
HD = 128
GSIZE = 4
TILE = 512
D = 5120
KVH = 4
QH = 32
GROUP = QH // KVH
NDP = 8
SHARD = 320
HALF = SHARD // 2
PIECE = TILE // NDP
EPS = 1e-06
VMEM_LIMIT = 62 * 1024 * 1024


def rope_arrays():
    half = HD // 2
    frequency = 1000000.0 ** (-np.arange(half, dtype=np.float64) / half)
    angles = np.arange(TILE, dtype=np.float64)[:, None] * frequency[None, :]
    cosine, sine = np.cos(angles), np.sin(angles)
    return (
        np.concatenate([cosine, cosine], axis=1).astype(np.float32),
        np.concatenate([-sine, sine], axis=1).astype(np.float32),
    )


def place():
    dp, fs = lax.axis_index("dp"), lax.axis_index("fsdp")
    return dp, fs, dp // 2, dp % 2, fs // 4, fs % 4


def remote(src, dst, send, recv, device):
    return pltpu.make_async_remote_copy(
        src_ref=src, dst_ref=dst, send_sem=send, recv_sem=recv, device_id=device, device_id_type=MESH
    )


def entry_barrier(peers):
    barrier = pltpu.get_barrier_semaphore()
    for peer in peers:
        pl.semaphore_signal(barrier, inc=1, device_id=peer, device_id_type=MESH)
    pl.semaphore_wait(barrier, len(peers))


def match(labels_ref, values_ref, label):
    found = jnp.int32(0)
    for r in range(NDP):
        found = jnp.where(labels_ref[0, r] == label, values_ref[0, r], found)
    return found


def swap_lanes(values):
    return pltpu.roll(values, HD // 2, axis=1)


class Sends:
    def __init__(self):
        self.pending = []

    def start(self, *args, group=None):
        copy = remote(*args)
        copy.start()
        self.pending.append((group, copy))

    def drain(self, group=None):
        rest = []
        for name, copy in self.pending:
            if group is None or name == group:
                copy.wait_send()
            else:
                rest.append((name, copy))
        self.pending = rest


HEADS = 4
QUADS = QH // HEADS


def layer_kernel(
    rewards_ref, length_ref, owner_ref, trainer_ref,
    x_hbm, kw_hbm, vw_hbm, q_hbm, og_hbm,
    qgain_ref, kgain_ref, cos_ref, sin_ref, cost_ref, sint_ref,
    hidden_hbm, dq_hbm, outk_ref, outv_ref, gq_out, gk_out,
    x_v, w_v, xt_v, tile_v, om0, om1, om2, om3, out_v, raw_v,
    q_in, og_in, dq_v, kv_v, kt_v, vt_v, acc_k, acc_v, acc_gain, wide_gain, coef_v,
    mid0, mid1, mid2, mid3, back_v, g_v, dw_v, give_v, pair_v, r1_v, r2_v, q_v, f_v, r7_v, full_v,
    gain_v, gain_r,
    load_sem, head_sem, ag_send, ag_recv, gx_send, gx_recv, ex_send, ex_recv, rs_send, rs_recv,
    x_send, x_recv, gn_send, gn_recv,
):
    out_mids = (om0, om1, om2, om3)
    mids = (mid0, mid1, mid2, mid3)
    dp, fs, cx, core, y, z = place()
    sibling = (dp + 1 - 2 * core, fs)

    def at(dy, dz):
        return (dp, ((y + dy) % 4) * 4 + (z + dz) % 4)

    peers = [((dp + k) % NDP, fs) for k in range(1, NDP)]
    peers += [at(k, 0) for k in range(1, 4)] + [at(0, k) for k in range(1, 4)]
    load_x = pltpu.make_async_copy(x_hbm, x_v, load_sem.at[KVH])

    def load_w(h, source):
        return pltpu.make_async_copy(
            source.at[:, pl.ds(h * HD, HD)], w_v.at[core, h, y, z], load_sem.at[h]
        )

    for h in range(KVH):
        @pl.when(core == 0)
        def _():
            load_w(h, kw_hbm).start()

        @pl.when(core == 1)
        def _():
            load_w(h, vw_hbm).start()

    load_x.start()
    entry_barrier(peers)
    for h in range(KVH):
        load_w(h, kw_hbm).wait()
    sends = Sends()

    def block(h, s, d1, d2, low, rows):
        dy, dz = (d1, d2) if s == 0 else (d2, d1)
        return w_v.at[core, h, (y + dy) % 4, (z + dz) % 4, pl.ds(s * HALF + low, rows), :]

    def ag_ahead(s, axis, step):
        return at(step, 0) if (s == 0) == (axis == 1) else at(0, step)

    def pass_on(h, s, axis, step, ref, slot):
        sends.start(ref, ref, ag_send.at[h, s, slot], ag_recv.at[h, s, slot], ag_ahead(s, axis, step))

    def got(h, s, ref, slot):
        remote(ref, ref, ag_send.at[h, s, slot], ag_recv.at[h, s, slot], sibling).wait_recv()

    def spread_block(h, s, b):
        ref = block(h, s, b, 0, 0, HALF)
        for step in (1, 3, 2):
            pass_on(h, s, 2, step, ref, 2 + 3 * b + step)

    def own(h):
        for s in range(2):
            ref = block(h, s, 0, 0, 0, HALF)
            for step in (1, 3, 2):
                pass_on(h, s, 1, step, ref, step - 1)
        for s in range(2):
            spread_block(h, s, 0)

    def near_blocks(h):
        for step in (1, 3, 2):
            for s in range(2):
                got(h, s, block(h, s, 4 - step, 0, 0, HALF), step - 1)
                spread_block(h, s, 4 - step)

    def share(h):
        for b in range(4):
            for s in range(2):
                for step in (1, 3, 2):
                    got(h, s, block(h, s, b, 4 - step, 0, HALF), 2 + 3 * b + step)
        sends.start(
            w_v.at[core, h], w_v.at[core, h], gx_send.at[h, 0, 0], gx_recv.at[h, 0, 0], sibling
        )

    def project(h):
        other = w_v.at[1 - core, h]
        remote(other, other, gx_send.at[h, 0, 0], gx_recv.at[h, 0, 0], sibling).wait_recv()
        @pl.loop(0, 2)
        def _(part):
            rows = pl.ds(pl.multiple_of(part * 256, 256), 256)
            weights = jnp.concatenate(
                [w_v[0, h].reshape(D, HD), w_v[1, h].reshape(D, HD)], axis=1
            )
            both = jnp.dot(x_v[rows, :], weights, preferred_element_type=F32)
            raw = both[:, :HD]
            raw_v[h, rows, :] = raw
            scale = lax.rsqrt(jnp.mean(raw * raw, axis=1, keepdims=True) + EPS)
            normed = raw * scale * kgain_ref[...]
            rot = normed * cos_ref[rows, :] + swap_lanes(normed) * sin_ref[rows, :]
            tile_v[h, rows, :] = jnp.concatenate([rot, both[:, HD:]], axis=1).astype(BF)

        for k in range(1, NDP):
            to = (dp + k) % NDP
            sends.start(
                tile_v.at[h, pl.ds(to * PIECE, PIECE), :], out_mids[h].at[dp],
                gx_send.at[h, 0, k], gx_recv.at[h, 0, k], (to, fs), group=("tile", h),
            )
        out_mids[h][dp] = tile_v[h, pl.ds(pl.multiple_of(dp * PIECE, PIECE), PIECE), :]

    def give(h):
        for k in range(1, NDP):
            ref = out_mids[h].at[(dp + NDP - k) % NDP]
            remote(ref, ref, gx_send.at[h, 0, k], gx_recv.at[h, 0, k], sibling).wait_recv()
        for k in range(NDP):
            to = (dp + k) % NDP
            out_v[h, k] = out_mids[h][match(trainer_ref, owner_ref, to)]
            ref = kv_v.at[h, pl.ds(dp * PIECE, PIECE), :]
            if k == 0:
                kv_v[h, pl.ds(pl.multiple_of(dp * PIECE, PIECE), PIECE), :] = out_v[h, k]
            else:
                sends.start(
                    out_v.at[h, k], ref, gx_send.at[h, 1, k], gx_recv.at[h, 1, k], (to, fs),
                    group=("out", h),
                )

    def arrive(h):
        for k in range(1, NDP):
            ref = kv_v.at[h, pl.ds(((dp + NDP - k) % NDP) * PIECE, PIECE), :]
            remote(ref, ref, gx_send.at[h, 1, k], gx_recv.at[h, 1, k], sibling).wait_recv()

    def turn(h):
        if h == 0:
            load_x.wait()

        step = D // KVH
        xt_v[h * step:(h + 1) * step, :] = x_v[:, h * step:(h + 1) * step].T

    width = HEADS * HD

    def load_heads(quad):
        columns, slot = pl.ds(quad * width, width), quad % 2
        return (
            pltpu.make_async_copy(q_hbm.at[:, columns], q_in.at[slot], head_sem.at[0, slot]),
            pltpu.make_async_copy(og_hbm.at[:, columns], og_in.at[slot], head_sem.at[1, slot]),
        )

    def store_heads(quad):
        columns, slot = pl.ds(quad * width, width), quad % 2
        return pltpu.make_async_copy(dq_v.at[slot], dq_hbm.at[:, columns], head_sem.at[2, slot])

    for copy in load_heads(0):
        copy.start()

    acc_gain[...] = jnp.zeros_like(acc_gain)
    column = jnp.broadcast_to(qgain_ref[...], (HD, HD)).T
    wide_gain[...] = jnp.concatenate([column] * (TILE // HD), axis=1)
    length, factor = jnp.int32(0), jnp.float32(0.0)
    for r in range(NDP):
        group = (r // GSIZE) * GSIZE
        total = rewards_ref[0, group]
        for member in range(1, GSIZE):
            total = total + rewards_ref[0, group + member]
        mine = trainer_ref[0, r] == dp
        length = jnp.where(mine, length_ref[0, r], length)
        factor = jnp.where(mine, rewards_ref[0, r] - total * (1.0 / GSIZE), factor)
    position = lax.broadcasted_iota(jnp.int32, (1, TILE), 1)
    coef_v[...] = jnp.where(position < length, factor, 0.0)
    half = HD // 2

    def swap(values):
        return jnp.concatenate([values[half:], values[:half]], axis=0)

    contract_lanes = (((1,), (1,)), ((), ()))

    def attend(quad):
        h, slot = quad // 2, quad % 2
        if slot == 0:
            kt_v[...] = kv_v[h, :, :HD].T
            vt_v[...] = kv_v[h, :, HD:].T
            acc_k[...] = jnp.zeros_like(acc_k)
            acc_v[...] = jnp.zeros_like(acc_v)
        for copy in load_heads(quad):
            copy.wait()
        if quad + 1 < QUADS:
            for copy in load_heads(quad + 1):
                copy.start()
        if quad >= 2:
            store_heads(quad - 2).wait()
        cosine, sine, gain = cost_ref[...], sint_ref[...], wide_gain[...]
        key_row = lax.broadcasted_iota(jnp.int32, (TILE, TILE), 0)
        query_lane = lax.broadcasted_iota(jnp.int32, (TILE, TILE), 1)
        causal = key_row <= query_lane
        for head in range(HEADS):
            columns = slice(head * HD, (head + 1) * HD)
            raw = q_in[slot, :, columns].T.astype(F32)
            scale = lax.rsqrt(jnp.mean(raw * raw, axis=0, keepdims=True) + EPS)
            unit = raw * scale
            normed = unit * gain
            rot = normed * cosine + swap(normed) * sine
            query = (rot * (math.log2(math.e) / math.sqrt(HD))).astype(BF)
            weighted = (og_in[slot, :, columns].T.astype(F32) * coef_v[...]).astype(BF).astype(F32)
            scores = jnp.dot(kv_v[h, :, :HD], query, preferred_element_type=F32)
            weight = jnp.where(causal, jnp.exp2(scores), 0.0)
            low = weight.astype(BF)
            inverse = 1.0 / jnp.sum(weight, axis=0, keepdims=True)
            attended = jnp.dot(vt_v[...], low, preferred_element_type=F32) * inverse
            scaled = (weighted * inverse).astype(BF)
            dotted = jnp.sum(scaled.astype(F32) * attended, axis=0, keepdims=True)
            grad_probs = jnp.dot(kv_v[h, :, HD:], scaled, preferred_element_type=F32)
            grad_scores = (weight * (grad_probs - dotted)).astype(BF)
            acc_v[...] += lax.dot_general(low, scaled, contract_lanes, preferred_element_type=F32)
            acc_k[...] += lax.dot_general(
                grad_scores, query, contract_lanes, preferred_element_type=F32
            )
            grad_rot = jnp.dot(kt_v[...], grad_scores, preferred_element_type=F32) * (
                1.0 / math.sqrt(HD)
            )
            grad_normed = grad_rot * cosine - swap(grad_rot) * sine
            terms = grad_normed * unit
            acc_gain[...] += (
                terms[:, :128] + terms[:, 128:256] + terms[:, 256:384] + terms[:, 384:]
            )
            mean = jnp.mean(terms * gain, axis=0, keepdims=True)
            dq_v[slot, :, columns] = (scale * (grad_normed * gain - unit * mean)).astype(BF).T
        store_heads(quad).start()
        if slot == 1:
            sends.drain(("tile", h))
            tile_v[h, :, :HD] = (acc_k[...] * math.log(2.0)).astype(BF)
            tile_v[h, :, HD:] = acc_v[...].astype(BF)

    def spread(h):
        for k in range(1, NDP):
            to = (dp + k) % NDP
            sends.start(
                tile_v.at[h, pl.ds(to * PIECE, PIECE), :], mids[h].at[dp],
                ex_send.at[h, 0, k], ex_recv.at[h, 0, k], (to, fs),
            )

        mids[h][dp] = tile_v[h, pl.ds(pl.multiple_of(dp * PIECE, PIECE), PIECE), :]

    def forward(h):
        sends.drain(("out", h))
        for k in range(1, NDP):
            ref = mids[h].at[(dp + NDP - k) % NDP]
            remote(ref, ref, ex_send.at[h, 0, k], ex_recv.at[h, 0, k], sibling).wait_recv()
        for k in range(NDP):
            to = (dp + k) % NDP
            if k == 0:
                back_v[h, dp] = mids[h][match(owner_ref, trainer_ref, to)]
            else:
                out_v[h, k] = mids[h][match(owner_ref, trainer_ref, to)]
                sends.start(
                    out_v.at[h, k], back_v.at[h, dp],
                    ex_send.at[h, 1, k], ex_recv.at[h, 1, k], (to, fs),
                )

    gain_parts = []

    def multiply(h):
        for k in range(1, NDP):
            ref = back_v.at[h, (dp + NDP - k) % NDP]
            remote(ref, ref, ex_send.at[h, 1, k], ex_recv.at[h, 1, k], sibling).wait_recv()
        grads = back_v[h].reshape(TILE, 2 * HD)
        grad_rot = grads[:, :HD].astype(F32)
        raw = raw_v[h]
        scale = lax.rsqrt(jnp.mean(raw * raw, axis=1, keepdims=True) + EPS)
        unit = raw * scale
        normed = grad_rot * cos_ref[...] - swap_lanes(grad_rot) * sin_ref[...]
        terms = normed * unit
        gain_parts.append(jnp.sum(terms, axis=0, keepdims=True))
        gained = normed * kgain_ref[...]
        mean = jnp.mean(gained * unit, axis=1, keepdims=True)
        own = slice(2 * HD * h, 2 * HD * h + 2 * HD)
        key_grads = (scale * (gained - unit * mean)).astype(BF)
        g_v[:, own] = jnp.concatenate([key_grads, grads[:, HD:]], axis=1)

        if h >= 2:
            sends.drain(("give", h - 2))

        @pl.loop(0, 4)
        def _(sy):
            start = pl.multiple_of(sy * 4 * SHARD, 4 * SHARD)
            part = jnp.dot(
                xt_v[pl.ds(start, 4 * SHARD), :], g_v[:, own], preferred_element_type=F32
            ).astype(BF)
            first, second = part[:, :HD], part[:, HD:]
            mine = jnp.where(core == 0, first, second)
            other = jnp.where(core == 0, second, first)
            for sz in range(4):
                low, high = sz * SHARD, sz * SHARD + HALF
                dw_v[h, 0, sz, sy] = mine[low:high]
                dw_v[h, 1, sy, sz] = mine[high:low + SHARD]
                give_v[h % 2, 0, sz, sy] = other[low:high]
                give_v[h % 2, 1, sy, sz] = other[high:low + SHARD]

        for s in range(2):
            sends.start(
                give_v.at[h % 2, s], pair_v.at[h, s],
                rs_send.at[h, s, 0], rs_recv.at[h, s, 0], sibling, group=("give", h),
            )

    def me(s, axis):
        return z if (s == 0) == (axis == 1) else y

    def ahead(s, axis, step):
        return at(0, step) if (s == 0) == (axis == 1) else at(step, 0)

    def send(h, s, slot, src, dst, axis, step):
        sends.start(src, dst, rs_send.at[h, s, slot], rs_recv.at[h, s, slot], ahead(s, axis, step))

    def landed(h, s, slot, ref):
        remote(ref, ref, rs_send.at[h, s, slot], rs_recv.at[h, s, slot], sibling).wait_recv()

    def add(ref, *others):
        total = ref[...].astype(F32)
        for other in others:
            total = total + other[...].astype(F32)
        ref[...] = total.astype(BF)

    def pair(h):
        for s in range(2):
            landed(h, s, 0, pair_v.at[h, s])
            mine = dw_v.at[h, s]
            for step in (2, 1, 3, 0):
                index = (me(s, 1) + step) % 4
                add(mine.at[index], pair_v.at[h, s, index])
                if step:
                    send(h, s, step, mine.at[index], r1_v.at[h, s, step - 1], 1, step)

    def cross(h):
        for s in range(2):
            for step in (1, 3, 2):
                landed(h, s, step, r1_v.at[h, s, step - 1])
            total = dw_v[h, s, me(s, 1)].astype(F32)
            for k in range(3):
                total = total + r1_v[h, s, k].astype(F32)
            q_v[h, s] = total.astype(BF)
            for step in (2, 1, 3):
                index = (me(s, 2) + step) % 4
                send(h, s, 3 + step, q_v.at[h, s, index], r2_v.at[h, s, step - 1], 2, step)

    def along_x(h):
        for s in range(2):
            for step in (1, 3, 2):
                landed(h, s, 3 + step, r2_v.at[h, s, step - 1])
            total = q_v[h, s, me(s, 2)].astype(F32)
            for k in range(3):
                total = total + r2_v[h, s, k].astype(F32)
            f_v[h, s * HALF:(s + 1) * HALF] = total.astype(BF)
        for k in range(1, 4):
            to = (cx + k) % 4
            sends.start(
                f_v.at[h, pl.ds(to * 80, 80), :], r7_v.at[h, k - 1],
                x_send.at[h, k - 1], x_recv.at[h, k - 1], (to * 2 + core, fs),
            )

    def spread_x(h):
        for k in range(1, 4):
            ref = r7_v.at[h, k - 1]
            remote(ref, ref, x_send.at[h, k - 1], x_recv.at[h, k - 1], sibling).wait_recv()
        rows = pl.ds(pl.multiple_of(cx * 80, 80), 80)
        total = f_v[h, rows, :].astype(F32)
        for k in range(3):
            total = total + r7_v[h, k].astype(F32)
        full_v[h, core, rows, :] = total.astype(BF)
        for k in range(1, NDP):
            ref = full_v.at[h, core, rows, :]
            sends.start(ref, ref, x_send.at[h, 2 + k], x_recv.at[h, 2 + k], ((dp + k) % NDP, fs))

    def finish(h):
        for k in range(1, NDP):
            source = (dp + NDP - k) % NDP
            ref = full_v.at[h, source % 2, pl.ds((source // 2) * 80, 80), :]
            remote(ref, ref, x_send.at[h, 2 + k], x_recv.at[h, 2 + k], sibling).wait_recv()
        outk_ref[:, h * HD:(h + 1) * HD] = full_v[h, 0].astype(F32)
        outv_ref[:, h * HD:(h + 1) * HD] = full_v[h, 1].astype(F32)

    groups = [
        (0, [((dp + k) % NDP, fs) for k in range(1, NDP)]),
        (7, [at(k, 0) for k in range(1, 4)]),
        (10, [at(0, k) for k in range(1, 4)]),
    ]

    def gains_out(stage):
        base, targets = groups[stage]
        for k, target in enumerate(targets):
            sends.start(
                gain_v.at[stage], gain_r.at[base + k], gn_send.at[base + k], gn_recv.at[base + k],
                target,
            )

    def gains_in(stage):
        base, targets = groups[stage]
        total = gain_v[stage]
        for k in range(len(targets)):
            ref = gain_r.at[base + k]
            remote(ref, ref, gn_send.at[base + k], gn_recv.at[base + k], sibling).wait_recv()
            total = total + gain_r[base + k]
        gain_v[stage + 1] = total

    def gains(stage):
        if stage == 0:
            row = lax.broadcasted_iota(jnp.int32, (8, HD), 0)
            keys = gain_parts[0] + gain_parts[1] + gain_parts[2] + gain_parts[3]
            queries = jnp.sum(acc_gain[...].T, axis=0, keepdims=True)
            gain_v[0] = jnp.where(row == 0, queries, jnp.where(row == 1, keys, 0.0))
        else:
            gains_in(stage - 1)
        if stage < 3:
            gains_out(stage)
        else:
            gq_out[...] = gain_v[3, 0:1]
            gk_out[...] = gain_v[3, 1:2]

    def then_gains(stage_function, stage):
        def both(h):
            stage_function(h)
            if h == KVH - 1:
                gains(stage)

        return both

    stages = [
        spread, forward, then_gains(multiply, 0), then_gains(pair, 1), then_gains(cross, 2),
        then_gains(along_x, 3), spread_x, finish,
    ]
    stores = []

    def hidden(part):
        wide = D // 4
        columns = slice(part * wide, (part + 1) * wide)
        weights = jnp.concatenate(
            [w_v[c, h, part].reshape(wide, HD) for h in range(KVH) for c in range(2)], axis=1
        )
        x_v[:, columns] = lax.dot_general(
            g_v[...], weights, contract_lanes, preferred_element_type=F32
        ).astype(BF)
        copy = pltpu.make_async_copy(
            x_v.at[:, pl.ds(part * wide, wide)], hidden_hbm.at[:, pl.ds(part * wide, wide)],
            load_sem.at[KVH + 1 + part],
        )
        copy.start()
        stores.append(copy)

    out_stages = [own, near_blocks, share, project, give, arrive]
    begin = len(out_stages)
    last = begin + 2 * KVH - 1
    for tick in range(last + len(stages)):
        if 0 <= tick - begin < QUADS:
            attend(tick - begin)
        for stage in (own, give, near_blocks, share, project, arrive):
            for h in range(KVH):
                if tick - 2 * h == out_stages.index(stage):
                    stage(h)
        for h in reversed(range(KVH)):
            step = tick - (begin + 2 * h + 1)
            if 0 <= step < len(stages):
                stages[step](h)
        if 1 <= tick <= KVH:
            turn(tick - 1)
        for part in {2: (0,), 3: (1, 2), 4: (3,)}.get(tick - last, ()):
            hidden(part)
    sends.drain()
    for quad in (QUADS - 2, QUADS - 1):
        store_heads(quad).wait()
    for copy in stores:
        copy.wait()


def layer_call(*operands):
    any_spec = pl.BlockSpec(memory_space=pl.ANY)
    vmem_spec = pl.BlockSpec(memory_space=pltpu.VMEM)
    heads = pltpu.VMEM((2, TILE, HEADS * HD), BF)
    tiles = pltpu.VMEM((KVH, TILE, 2 * HD), BF)
    pieces = pltpu.VMEM((NDP, PIECE, 2 * HD), BF)
    all_pieces = pltpu.VMEM((KVH, NDP, PIECE, 2 * HD), BF)
    dma = pltpu.SemaphoreType.DMA
    return pl.pallas_call(
        layer_kernel,
        out_shape=(
            jax.ShapeDtypeStruct((TILE, D), BF),
            jax.ShapeDtypeStruct((TILE, QH * HD), BF),
            jax.ShapeDtypeStruct((SHARD, KVH * HD), F32),
            jax.ShapeDtypeStruct((SHARD, KVH * HD), F32),
            jax.ShapeDtypeStruct((1, HD), F32),
            jax.ShapeDtypeStruct((1, HD), F32),
        ),
        in_specs=[pl.BlockSpec(memory_space=pltpu.SMEM)] * 4 + [any_spec] * 5 + [vmem_spec] * 6,
        out_specs=(any_spec,) * 2 + (vmem_spec,) * 4,
        scratch_shapes=[
            pltpu.VMEM((TILE, D), BF),
            pltpu.VMEM((2, KVH, 4, 4, SHARD, HD), BF),
            pltpu.VMEM((D, TILE), BF),
            tiles, pieces, pieces, pieces, pieces, all_pieces,
            pltpu.VMEM((KVH, TILE, HD), F32),
            heads, heads, heads, tiles,
            pltpu.VMEM((HD, TILE), BF),
            pltpu.VMEM((HD, TILE), BF),
            pltpu.VMEM((TILE, HD), F32),
            pltpu.VMEM((TILE, HD), F32),
            pltpu.VMEM((HD, HD), F32),
            pltpu.VMEM((HD, TILE), F32),
            pltpu.VMEM((1, TILE), F32),
            pieces, pieces, pieces, pieces, all_pieces,
            pltpu.VMEM((TILE, 2 * KVH * HD), BF),
            pltpu.VMEM((KVH, 2, 4, 4, HALF, HD), BF),
            pltpu.VMEM((2, 2, 4, 4, HALF, HD), BF),
            pltpu.VMEM((KVH, 2, 4, 4, HALF, HD), BF),
            pltpu.VMEM((KVH, 2, 3, 4, HALF, HD), BF),
            pltpu.VMEM((KVH, 2, 3, HALF, HD), BF),
            pltpu.VMEM((KVH, 2, 4, HALF, HD), BF),
            pltpu.VMEM((KVH, SHARD, HD), BF),
            pltpu.VMEM((KVH, 3, 80, HD), BF),
            pltpu.VMEM((KVH, 2, SHARD, HD), BF),
            pltpu.VMEM((4, 8, HD), F32),
            pltpu.VMEM((13, 8, HD), F32),
            dma((KVH + 5,)), dma((3, 2)),
            dma((KVH, 2, 15)), dma((KVH, 2, 15)),
            dma((KVH, 2, NDP)), dma((KVH, 2, NDP)),
            dma((KVH, 2, NDP)), dma((KVH, 2, NDP)),
            dma((KVH, 2, 7)), dma((KVH, 2, 7)),
            dma((KVH, 10)), dma((KVH, 10)),
            dma((13,)), dma((13,)),
        ],
        compiler_params=pltpu.CompilerParams(
            collective_id=0, has_side_effects=True, vmem_limit_bytes=VMEM_LIMIT
        ),
        name="layer_backward",
    )(*operands)


def per_device(
    rollout_hidden, key_weight, value_weight, key_gain, query_gain, queries, out_grad, rewards,
    response_lengths, rollout_owner, train_shard, pack_offsets,
):
    del pack_offsets
    cosine, sine = rope_arrays()
    d_hidden, d_queries, grad_key_weight, grad_value_weight, query_gain_grad, key_gain_grad = (
        layer_call(
            rewards, response_lengths, rollout_owner, train_shard,
            rollout_hidden, key_weight, value_weight, queries, out_grad,
            query_gain.reshape(1, HD), key_gain.reshape(1, HD),
            cosine, sine, np.ascontiguousarray(cosine.T), np.ascontiguousarray(sine.T),
        )
    )
    return (
        d_hidden, d_queries, grad_key_weight, grad_value_weight,
        query_gain_grad.reshape(HD), key_gain_grad.reshape(HD),
    )


def solution(mesh):
    rows, split = P(("dp", "fsdp"), None), P("fsdp", None)
    return jax.shard_map(
        per_device,
        mesh=mesh,
        in_specs=(rows, split, split, P(), P(), rows, rows, split, split, split, split, split),
        out_specs=(rows, rows, split, split, P(), P()),
        check_vma=False,
    )
```
